512 devices in a mesh: depth: 32 (over z, core), lat: 16 (over x, y).
Axes of the slice: x: 4, y: 4, z: 16, core: 2. Of those that a mesh axis runs over, the one named last changes fastest.
Arguments:
- checkpoint: float32 [9, 256, 256, 256], P(None, 'depth', 'lat'), may hold values from -6 to 6
- end_cotangent: float32 [9, 256, 256, 256], P(None, 'depth', 'lat'), may hold values from -6 to 6
- buoyancy: float32 [256, 256, 256], P('depth', 'lat'), may hold values from 0.15 to 0.4
- moduli: float32 [2, 256, 256, 256], P(None, 'depth', 'lat'), may hold values from 0.1 to 0.35
- yield_radius: float32 [256, 256, 256], P('depth', 'lat'), may hold values from 0.3 to 1.5
- mask: int32 [3, 256, 256, 256], P(None, 'depth', 'lat'), may hold values 0 or 1
- footprint: int32 [256, 256], P('lat'), may hold values from 0 to 63
- amplitude: float32 [64], replicated, may hold values from 0.5 to 2
Outputs:
- adjoint_state: float32 [9, 256, 256, 256], P(None, 'depth', 'lat')
- pulse_grad: float32 [64], replicated
The draws below stay inside these ranges and needn't reach their ends.
All inputs are finite; a program needn't handle non-finite values. No bound on the sum of `mask` on one device may be relied on, other than what follows from the above.
Results may differ from the reference program's by a relative error of at most 0.00012.
Values sent between devices are 32-bit elements; how exact they have to be, the bound alone decides.
A program may use at most 64 MiB of HBM per device.

```python
import math
import jax
import jax.numpy as jnp

NY = 256
STEPS = 3
PULSES = 64
NZ = 256
NX = 256


def touch_ends(values, rng, smallest, largest):
    spot = [jax.random.randint(jax.random.fold_in(rng, axis), (), 0, length) for axis, length in enumerate(values.shape)]
    longest = values.shape.index(max(values.shape))
    beside = spot[:longest] + [(spot[longest] + 1) % values.shape[longest]] + spot[longest + 1:]
    return values.at[tuple(spot)].set(smallest).at[tuple(beside)].set(largest)


def level_of(key, shape, shards, low, high):
    def one(position, shards_of):
        draws = jax.random.uniform(jax.random.fold_in(jax.random.fold_in(key, 6), position), (shards_of,), jnp.float32, low / len(shards), high / len(shards))
        return jnp.repeat(jnp.exp(draws), shape[position] // shards_of).reshape((-1,) + (1,) * (len(shape) - position - 1))

    gain = one(*shards[0])
    for cut in shards[1:]:
        gain = gain * one(*cut)
    return gain


def centred(rng, shape, scale, most, cuts=(), kind=jnp.bfloat16):
    entries = jax.random.normal(rng, shape, jnp.float32) * scale
    if len(cuts) > 0:
        entries = level_of(rng, shape, cuts, -0.22, 0.18) * entries
    return jnp.clip(entries, min=-most, max=most).astype(kind)


def setup_inputs(seed: int = 0) -> dict:
    arg_keys = jax.random.split(jax.random.key(seed), 9)
    checkpoint = centred(arg_keys[0], (9, NZ, NX, NY), 1.0, 6.0, ((1, 32), (2, 16)), jnp.float32)
    end_cotangent = centred(arg_keys[1], (9, NZ, NX, NY), 1.0, 6.0, ((1, 32), (2, 16)), jnp.float32)
    buoyancy = jnp.clip(jnp.exp(math.log(0.4) - 0.98082923 * jax.random.uniform(arg_keys[2], (NZ, NX, NY), jnp.float32) ** level_of(arg_keys[2], (NZ, NX, NY), ((0, 32), (1, 16)), -0.2, 0.2)), 0.15, 0.4)
    moduli = jnp.clip(jnp.exp(math.log(0.35) - 1.2527629 * jax.random.uniform(arg_keys[3], (2, NZ, NX, NY), jnp.float32) ** level_of(arg_keys[3], (2, NZ, NX, NY), ((1, 32), (2, 16)), -0.2, 0.2)), 0.1, 0.35)
    yield_radius = jnp.clip(jnp.exp(math.log(1.5) - 1.60943787 * jax.random.uniform(arg_keys[4], (NZ, NX, NY), jnp.float32) ** level_of(arg_keys[4], (NZ, NX, NY), ((0, 32), (1, 16)), -0.2, 0.2)), 0.3, 1.5)
    mask = touch_ends((jax.random.randint(arg_keys[5], (STEPS, NZ, NX, NY), 0, 2) < 1).astype(jnp.int32), jax.random.fold_in(arg_keys[5], 1), 0, 1)
    footprint = touch_ends(jax.random.randint(arg_keys[6], (NX, NY), 0, PULSES), jax.random.fold_in(arg_keys[6], 1), 0, PULSES - 1).astype(jnp.int32)
    amplitude = jnp.clip(jnp.exp(jax.random.uniform(arg_keys[7], (PULSES,), jnp.float32, math.log(0.5), math.log(2.0))), 0.5, 2.0)
    return {"checkpoint": checkpoint, "end_cotangent": end_cotangent, "buoyancy": buoyancy, "moduli": moduli, "yield_radius": yield_radius, "mask": mask, "footprint": footprint, "amplitude": amplitude}


def plus_z(field):
    return field[2:, 1:-1] - field[1:-1, 1:-1]

def minus_z(field):
    return field[1:-1, 1:-1] - field[:-2, 1:-1]

def plus_x(field):
    return field[1:-1, 2:] - field[1:-1, 1:-1]

def minus_x(field):
    return field[1:-1, 1:-1] - field[1:-1, :-2]

def plus_y(field):
    middle = field[1:-1, 1:-1]
    return jnp.concatenate([middle[..., 1:], jnp.zeros_like(middle[..., :1])], -1) - middle

def minus_y(field):
    middle = field[1:-1, 1:-1]
    return middle - jnp.concatenate([jnp.zeros_like(middle[..., :1]), middle[..., :-1]], -1)

def divergence(tensor):
    return jnp.stack([plus_x(tensor[0]) + minus_y(tensor[3]) + minus_z(tensor[4]), minus_x(tensor[3]) + plus_y(tensor[1]) + minus_z(tensor[5]), minus_x(tensor[4]) + minus_y(tensor[5]) + plus_z(tensor[2])])

def gradient(vector):
    return jnp.stack([minus_x(vector[0]), minus_y(vector[1]), minus_z(vector[2]), plus_y(vector[0]) + plus_x(vector[1]), plus_z(vector[0]) + plus_x(vector[2]), plus_z(vector[1]) + plus_y(vector[2])])

def radial_return(stress, strain, lame, shear, limit, plastic):
    trace = strain[0] + strain[1] + strain[2]
    normal = [stress[a] + lame * trace + 2.0 * shear * strain[a] for a in range(3)]
    sheared = [stress[a] + shear * strain[a] for a in range(3, 6)]
    mean = (normal[0] + normal[1] + normal[2]) / 3.0
    devs = [normal[a] - mean for a in range(3)]
    qsq = devs[0] * devs[0] + devs[1] * devs[1] + devs[2] * devs[2] + 2.0 * (sheared[0] * sheared[0] + sheared[1] * sheared[1] + sheared[2] * sheared[2])
    factor = 1.0 - plastic + plastic * limit / jnp.sqrt(limit * limit + qsq)
    return jnp.stack([mean + factor * devs[0], mean + factor * devs[1], mean + factor * devs[2], factor * sheared[0], factor * sheared[1], factor * sheared[2]])

def pad_sides(stack):
    return jnp.pad(stack, ((0, 0), (1, 1), (1, 1), (0, 0)))

def reference(checkpoint, end_cotangent, buoyancy, moduli, yield_radius, mask, footprint, amplitude):
    load_map = amplitude[footprint]

    def advance(state, index):
        velocity = state[:3] + buoyancy * divergence(pad_sides(state[3:]))
        strain = gradient(pad_sides(velocity))
        plastic = mask[index].astype(jnp.float32)
        stress = radial_return(state[3:], strain, moduli[0], moduli[1], yield_radius, plastic)
        pulse = math.sin(math.pi * (index + 0.5) / STEPS)
        stress = stress.at[2, 0].add(pulse * load_map)
        return jnp.concatenate([velocity, stress], 0)
    history = []
    state = checkpoint
    for index in range(STEPS):
        history.append(state)
        state = advance(state, index)
    cotangent = end_cotangent
    totals = jnp.zeros((PULSES,), jnp.float32)
    flat_ids = footprint.reshape(-1)
    for index in reversed(range(STEPS)):
        pulse = math.sin(math.pi * (index + 0.5) / STEPS)
        totals = totals + pulse * jax.ops.segment_sum(cotangent[5, 0].reshape(-1), flat_ids, num_segments=PULSES)
        _, pull = jax.vjp(lambda current, index=index: advance(current, index), history[index])
        cotangent = pull(cotangent)[0]
    return (cotangent, totals * math.sqrt(PULSES / (NX * NY)))
```

```python
import functools
import math

import jax
import jax.numpy as jnp
from jax import lax
from jax.experimental import pallas as pl
from jax.experimental.pallas import tpu as pltpu
from jax.sharding import PartitionSpec as P

MESH = pl.DeviceIdType.MESH
F32 = jnp.float32

NZ_OWN = 8
NX_OWN = 16
GROUP = 24
LAYER = 2 * GROUP
BASE = 8
ROWS = BASE + (NZ_OWN + 4) * LAYER


def row_of(z, x, half=0):
    return BASE + LAYER * (z + 2) + GROUP * half + x


class Tile:
    def __init__(self, row, stride=1):
        self.row = row
        self.stride = stride

    def at(self, half, shift=0):
        start = self.row + GROUP * half + shift
        return pl.ds(start, 8) if self.stride == 1 else pl.ds(start, 8, self.stride)

    def load(self, ref, field, dz=0, dx=0):
        return [ref[field, self.at(half, LAYER * dz + dx), :] for half in range(2)]

    def store(self, ref, field, half, value):
        ref[field, self.at(half), :] = value


def y_shifts():
    lane = lax.broadcasted_iota(jnp.int32, (8, 128), 1)
    first = lane == 0
    last = lane == 127

    def before(pair):
        low, high = pltpu.roll(pair[0], 1, 1), pltpu.roll(pair[1], 1, 1)
        return [jnp.where(first, 0.0, low), jnp.where(first, low, high)]

    def after(pair):
        low, high = pltpu.roll(pair[0], 127, 1), pltpu.roll(pair[1], 127, 1)
        return [jnp.where(last, high, low), jnp.where(last, 0.0, high)]

    return before, after


def divergence(tile, ref):
    before, after = y_shifts()
    c = [tile.load(ref, k) for k in range(6)]
    xx_next = tile.load(ref, 0, dx=1)
    xy_prev = tile.load(ref, 3, dx=-1)
    xz_prev = tile.load(ref, 4, dx=-1)
    xz_up = tile.load(ref, 4, dz=-1)
    yz_up = tile.load(ref, 5, dz=-1)
    zz_down = tile.load(ref, 2, dz=1)
    xy_y = before(c[3])
    yz_y = before(c[5])
    yy_y = after(c[1])
    out = []
    for h in range(2):
        out.append(
            (
                (xx_next[h] - c[0][h]) + (c[3][h] - xy_y[h]) + (c[4][h] - xz_up[h]),
                (c[3][h] - xy_prev[h]) + (yy_y[h] - c[1][h]) + (c[5][h] - yz_up[h]),
                (c[4][h] - xz_prev[h]) + (c[5][h] - yz_y[h]) + (zz_down[h] - c[2][h]),
            )
        )
    return out


def gradient(tile, ref):
    before, after = y_shifts()
    w = [tile.load(ref, k) for k in range(3)]
    wx_prev = tile.load(ref, 0, dx=-1)
    wz_up = tile.load(ref, 2, dz=-1)
    wy_next = tile.load(ref, 1, dx=1)
    wz_next = tile.load(ref, 2, dx=1)
    wx_down = tile.load(ref, 0, dz=1)
    wy_down = tile.load(ref, 1, dz=1)
    wy_y = before(w[1])
    wx_y = after(w[0])
    wz_y = after(w[2])
    out = []
    for h in range(2):
        out.append(
            (
                w[0][h] - wx_prev[h],
                w[1][h] - wy_y[h],
                w[2][h] - wz_up[h],
                (wx_y[h] - w[0][h]) + (wy_next[h] - w[1][h]),
                (wx_down[h] - w[0][h]) + (wz_next[h] - w[2][h]),
                (wy_down[h] - w[1][h]) + (wz_y[h] - w[2][h]),
            )
        )
    return out


def trial(s, e, lame, shear, limit, plastic):
    volume = lame * (e[0] + e[1] + e[2])
    twice = 2.0 * shear
    normal = [s[a] + volume + twice * e[a] for a in range(3)]
    shears = [s[a] + shear * e[a] for a in range(3, 6)]
    mean = (normal[0] + normal[1] + normal[2]) * (1.0 / 3.0)
    devs = [normal[a] - mean for a in range(3)]
    qsq = (devs[0] * devs[0] + devs[1] * devs[1] + devs[2] * devs[2]) + 2.0 * (
        shears[0] * shears[0] + shears[1] * shears[1] + shears[2] * shears[2]
    )
    inverse = lax.rsqrt(limit * limit + qsq)
    scaled = plastic * limit * inverse
    factor = (1.0 - plastic) + scaled
    slope = scaled * (inverse * inverse)
    return mean, devs + shears, factor, slope


def pull_back(g, parts, factor, slope, lame, shear):
    along = (g[0] * parts[0] + g[1] * parts[1] + g[2] * parts[2]) + (
        g[3] * parts[3] + g[4] * parts[4] + g[5] * parts[5]
    )
    pull = slope * along
    pull_twice = pull + pull
    total = g[0] + g[1] + g[2]
    rest = (1.0 - factor) * (total * (1.0 / 3.0))
    twice = 2.0 * shear
    volume = lame * total
    stress = [factor * g[a] - pull * parts[a] + rest for a in range(3)]
    stress += [factor * g[a] - pull_twice * parts[a] for a in range(3, 6)]
    strain = [volume + twice * stress[a] for a in range(3)]
    strain += [shear * stress[a] for a in range(3, 6)]
    return stress, strain


TO_LOW = (0, 1, 2, 3, 4, 5)
TO_HIGH = (3, 4, 0, 1, 2, 5)
WIDE_LOW = ((0, 0, 16), (1, 0, 16), (2, 0, 16), (1, 1, 17), (2, 1, 17))
WIDE_HIGH = ((0, 15, -1), (1, 15, -1), (2, 15, -1), (0, 14, -2))
THIN_LOW = ((1, 0, 16), (2, 0, 16))
THIN_HIGH = ((0, 15, -1),)


def kernel(
    nd, nl, steps, pulses, wide_y,
    cp_in, ec_in, bu_in, mo_in, yi_in, ma_in, fp_ref, amp_ref,
    out_ref, pulse_ref,
    cp, ec, bu, mo, yi, ma,
    st, sp, co, vs, vb, hist, cf,
    load_map, q_map, fx_send, fx_low, fx_high, zs_low, zs_high, zc_low, zc_high, zm_low, zm_high,
    vx_send, vx_low, vx_high, cor_send, cor_recv,
    psum_buf, ysum_buf, xsum_buf, total_buf,
    in_sem, send_sem, recv_sem, far_sem,
):
    d = lax.axis_index("depth")
    l = lax.axis_index("lat")
    top = d == 0
    bottom = d == nd - 1
    has_low = l > 0
    has_high = l < nl - 1
    up = lax.rem(d + nd - 1, nd)
    down = lax.rem(d + 1, nd)
    low = jnp.maximum(l - 1, 0)
    high = jnp.minimum(l + 1, nl - 1)
    gains = [math.sin(math.pi * (n + 0.5) / steps) for n in range(steps)]

    loads = []
    for k, (source, target) in enumerate(((cp_in, cp), (mo_in, mo), (yi_in, yi), (ma_in, ma), (bu_in, bu), (ec_in, ec))):
        copy = pltpu.make_async_copy(source, target, in_sem.at[k])
        copy.start()
        loads.append(copy)

    barrier = pltpu.get_barrier_semaphore()

    def greet(dd, ll):
        pl.semaphore_signal(barrier, inc=1, device_id=(dd, ll), device_id_type=MESH)

    greet(up, l)
    greet(down, l)

    @pl.when(has_low)
    def _():
        greet(d, low)
        greet(up, low)
        greet(down, low)

    @pl.when(has_high)
    def _():
        greet(d, high)
        greet(up, high)
        greet(down, high)

    l_y = lax.rem(l, wide_y)
    l_x = l // wide_y
    n_x = nl // wide_y
    y_peers = [l_x * wide_y + lax.rem(l_y + k, wide_y) for k in range(1, wide_y)]
    x_peers = [lax.rem(l_x + k, n_x) * wide_y + l_y for k in range(1, n_x)]

    @pl.when(top)
    def _():
        for peer in y_peers + x_peers:
            greet(d, peer)

    ids = iter(range(1000))

    def remote(source, target, where):
        k = next(ids)
        return pltpu.make_async_remote_copy(
            src_ref=source, dst_ref=target, send_sem=send_sem.at[k], recv_sem=recv_sem.at[k],
            device_id=where, device_id_type=MESH,
        )

    def own(z, t, h):
        return (z, pl.ds(8 * t, 8), pl.ds(128 * h, 128))

    def stage(z, carry):
        for t in range(2):
            for h in range(2):
                place = pl.ds(row_of(z, 8 * t, h), 8)
                for k in range(6):
                    st[k, place, :] = cp[(3 + k,) + own(z, t, h)]
                cf[0, place, :] = mo[(0,) + own(z, t, h)]
                cf[1, place, :] = mo[(1,) + own(z, t, h)]
                cf[2, place, :] = yi[own(z, t, h)]
                for k in range(3):
                    cf[3 + k, place, :] = ma[(k,) + own(z, t, h)].astype(F32)
        return carry

    def stage_end(z, carry):
        for t in range(2):
            for h in range(2):
                place = pl.ds(row_of(z, 8 * t, h), 8)
                for k in range(6):
                    sp[k, place, :] = ec[(3 + k,) + own(z, t, h)]
        return carry

    for copy in loads[:4]:
        copy.wait()
    lax.fori_loop(0, NZ_OWN, stage, 0)

    load_map[...] = jnp.zeros_like(load_map)

    @pl.when(top)
    def _():
        for t in range(2):
            for h in range(2):
                foot = fp_ref[pl.ds(8 * t, 8), pl.ds(128 * h, 128)]

                def add(p, total, foot=foot):
                    return jnp.where(foot == p, amp_ref[p], total)

                load_map[pl.ds(BASE + GROUP * h + 8 * t, 8), :] = lax.fori_loop(
                    0, pulses, add, jnp.zeros((8, 128), F32), unroll=8
                )

    zero = jnp.zeros((8, 128), F32)

    @pl.when(jnp.logical_not(has_low))
    def _():
        fx_low[...] = jnp.zeros_like(fx_low)
        vx_low[...] = jnp.zeros_like(vx_low)
        for p in range(2 * steps - 1):
            cor_recv[p, 0] = zero
            cor_recv[p, 1] = zero

    @pl.when(jnp.logical_not(has_high))
    def _():
        fx_high[...] = jnp.zeros_like(fx_high)
        vx_high[...] = jnp.zeros_like(vx_high)
        for p in range(2 * steps - 1):
            cor_recv[p, 2] = zero
            cor_recv[p, 3] = zero

    def face(ref, field, x, h):
        return ref[field, pl.ds(row_of(0, x, h), NZ_OWN, LAYER), :]

    for side, order, x in ((0, TO_LOW, 0), (1, TO_HIGH, NX_OWN - 1)):
        for k, field in enumerate(order):
            for h in range(2):
                fx_send[side, 2 * k + h] = face(st, field, x, h)
        for k in range(6):
            for h in range(2):
                fx_send[side, 12 + 2 * k + h] = face(cf, k, x, h)
        for h in range(2):
            fx_send[side, 24, pl.ds(h, 1), :] = load_map[pl.ds(BASE + GROUP * h + x, 1), :]

    near = 2 + 3 * has_low.astype(jnp.int32) + 3 * has_high.astype(jnp.int32)
    pl.semaphore_wait(barrier, near + top.astype(jnp.int32) * (len(y_peers) + len(x_peers)))

    class Exchange:
        def __init__(self):
            self.depth, self.low, self.high = [], [], []

        def start(self):
            for copy in self.depth:
                copy.start()

            @pl.when(has_low)
            def _():
                for copy in self.low:
                    copy.start()

            @pl.when(has_high)
            def _():
                for copy in self.high:
                    copy.start()

        def wait_send(self):
            for copy in self.depth:
                copy.wait_send()

            @pl.when(has_low)
            def _():
                for copy in self.low:
                    copy.wait_send()

            @pl.when(has_high)
            def _():
                for copy in self.high:
                    copy.wait_send()

        def wait_recv(self):
            for copy in self.depth:
                copy.wait_recv()

            @pl.when(has_high)
            def _():
                for copy in self.low:
                    copy.wait_recv()

            @pl.when(has_low)
            def _():
                for copy in self.high:
                    copy.wait_recv()

    last = NZ_OWN - 1
    first_faces = Exchange()
    first_faces.depth = [
        remote(cp.at[pl.ds(7, 2), last], zs_low.at[pl.ds(4, 2)], (down, l)),
        remote(cp.at[pl.ds(5, 1), 0], zs_high.at[pl.ds(2, 1)], (up, l)),
    ]
    first_faces.low = [remote(fx_send.at[0, pl.ds(0, 2)], fx_high.at[pl.ds(0, 2)], (d, low))]
    first_faces.high = [remote(fx_send.at[1, pl.ds(0, 4)], fx_low.at[pl.ds(0, 4)], (d, high))]
    first_faces.start()
    rest = Exchange()
    rest.depth = [
        remote(cp.at[pl.ds(3, 4), last], zs_low.at[pl.ds(0, 4)], (down, l)),
        remote(mo.at[:, last], zc_low.at[pl.ds(0, 2)], (down, l)),
        remote(yi.at[pl.ds(last, 1)], zc_low.at[pl.ds(2, 1)], (down, l)),
        remote(ma.at[:, last], zm_low, (down, l)),
        remote(cp.at[pl.ds(3, 2), 0], zs_high.at[pl.ds(0, 2)], (up, l)),
        remote(cp.at[pl.ds(6, 3), 0], zs_high.at[pl.ds(3, 3)], (up, l)),
        remote(mo.at[:, 0], zc_high.at[pl.ds(0, 2)], (up, l)),
        remote(yi.at[pl.ds(0, 1)], zc_high.at[pl.ds(2, 1)], (up, l)),
        remote(ma.at[:, 0], zm_high, (up, l)),
    ]
    rest.low = [remote(fx_send.at[0, pl.ds(2, 23)], fx_high.at[pl.ds(2, 23)], (d, low))]
    rest.high = [remote(fx_send.at[1, pl.ds(4, 21)], fx_low.at[pl.ds(4, 21)], (d, high))]
    rest.start()

    for copy in loads[4:]:
        copy.wait()
    lax.fori_loop(0, NZ_OWN, stage_end, 0)
    for side, x in ((0, 0), (1, NX_OWN - 1)):
        for k in range(6):
            for h in range(2):
                fx_send[side, 25 + 2 * k + h] = face(sp, k, x, h)
    ends = Exchange()
    ends.depth = [
        remote(ec.at[pl.ds(3, 6), last], zs_low.at[pl.ds(6, 6)], (down, l)),
        remote(ec.at[pl.ds(3, 6), 0], zs_high.at[pl.ds(6, 6)], (up, l)),
    ]
    ends.low = [remote(fx_send.at[0, pl.ds(25, 12)], fx_high.at[pl.ds(25, 12)], (d, low))]
    ends.high = [remote(fx_send.at[1, pl.ds(25, 12)], fx_low.at[pl.ds(25, 12)], (d, high))]
    ends.start()

    def put_face(ref, field, x, h, value):
        ref[field, pl.ds(row_of(0, x, h), NZ_OWN, LAYER), :] = value

    def put_layer(ref, field, z, source, outside):
        for t in range(2):
            for h in range(2):
                value = source[pl.ds(8 * t, 8), pl.ds(128 * h, 128)].astype(F32)
                if outside is not None:
                    value = jnp.where(outside, 0.0, value)
                ref[field, pl.ds(row_of(z, 8 * t, h), 8), :] = value

    def put_stress(fields):
        for field in fields[0]:
            put_layer(st, field, -1, zs_low.at[field], top)
        for field in fields[1]:
            put_layer(st, field, NZ_OWN, zs_high.at[field], bottom)
        for field in fields[2]:
            for h in range(2):
                put_face(st, field, -1, h, fx_low[2 * TO_HIGH.index(field) + h])
        for field in fields[3]:
            for h in range(2):
                put_face(st, field, NX_OWN, h, fx_high[2 * TO_LOW.index(field) + h])

    inside_z = [jnp.logical_not(top), jnp.logical_not(bottom)]

    def everywhere(unit):
        def inner(z, carry):
            for t in range(2):
                unit(Tile(row_of(z, 8 * t)), None)
            return carry

        lax.fori_loop(0, NZ_OWN, inner, 0)

        def outer(i, carry):
            side = i // 2
            z = -1 + (NZ_OWN + 1) * side
            inside = jnp.where(side == 0, inside_z[0].astype(jnp.int32), inside_z[1].astype(jnp.int32)) > 0
            unit(Tile(row_of(z, 8 * lax.rem(i, 2))), inside)
            return carry

        lax.fori_loop(0, 4, outer, 0)
        unit(Tile(row_of(0, -1), LAYER), has_low)
        unit(Tile(row_of(0, NX_OWN), LAYER), has_high)

    def keep(inside, value):
        return value if inside is None else jnp.where(inside, value, 0.0)

    def coefficients(tile, n):
        return [tile.load(cf, k) for k in (0, 1, 2, 3 + n)]

    def forward_stress(n):
        v = vs.at[n]
        record = hist.at[n]

        def unit(tile, inside):
            e = gradient(tile, v)
            s = [tile.load(st, k) for k in range(6)]
            lame, shear, limit, plastic = coefficients(tile, n)
            for h in range(2):
                mean, parts, factor, slope = trial(
                    [s[k][h] for k in range(6)], e[h], lame[h], shear[h], limit[h], plastic[h]
                )
                for k in range(6):
                    value = factor * parts[k]
                    if k < 3:
                        value = mean + value
                    tile.store(st, k, h, keep(inside, value))
                    tile.store(record, k, h, parts[k])
                tile.store(record, 6, h, factor)
                tile.store(record, 7, h, slope)

        everywhere(unit)

        @pl.when(top)
        def _():
            for h in range(2):
                for x, count in ((-1, 1), (0, 8), (8, 8), (16, 1)):
                    place = pl.ds(row_of(0, x, h), count)
                    st[2, place, :] += gains[n] * load_map[pl.ds(BASE + GROUP * h + x, count), :]

    def turn():
        n = steps - 1
        v = vs.at[n]

        def unit(tile, inside):
            e = gradient(tile, v)
            s = [tile.load(st, k) for k in range(6)]
            g = [tile.load(sp, k) for k in range(6)]
            lame, shear, limit, plastic = coefficients(tile, n)
            for h in range(2):
                mean, parts, factor, slope = trial(
                    [s[k][h] for k in range(6)], e[h], lame[h], shear[h], limit[h], plastic[h]
                )
                stress, strain = pull_back([g[k][h] for k in range(6)], parts, factor, slope, lame[h], shear[h])
                for k in range(6):
                    tile.store(sp, k, h, stress[k])
                    tile.store(co, k, h, keep(inside, strain[k]))

        everywhere(unit)

    def backward_stress(n):
        w = vs.at[2 * steps - 2 - n]
        record = hist.at[n]

        def unit(tile, inside):
            back = gradient(tile, w)
            s = [tile.load(sp, k) for k in range(6)]
            kept = [tile.load(record, k) for k in range(8)]
            lame, shear = tile.load(cf, 0), tile.load(cf, 1)
            for h in range(2):
                g = [s[k][h] - back[h][k] for k in range(6)]
                stress, strain = pull_back(
                    g, [kept[k][h] for k in range(6)], kept[6][h], kept[7][h], lame[h], shear[h]
                )
                for k in range(6):
                    tile.store(sp, k, h, stress[k])
                    tile.store(co, k, h, keep(inside, strain[k]))

        everywhere(unit)

    def forward_velocity(n):
        def body(z, carry):
            for t in range(2):
                tile = Tile(row_of(z, 8 * t))
                div = divergence(tile, st)
                for h in range(2):
                    b = bu[own(z, t, h)]
                    for k in range(3):
                        old = cp[(k,) + own(z, t, h)] if n == 0 else vs[n - 1, k, tile.at(h), :]
                        vs[n, k, tile.at(h), :] = old + b * div[h][k]
            return carry

        lax.fori_loop(0, NZ_OWN, body, 0)

    def backward_velocity(n):
        slot = 2 * steps - 1 - n

        def body(z, carry):
            for t in range(2):
                tile = Tile(row_of(z, 8 * t))
                div = divergence(tile, co)
                for h in range(2):
                    b = bu[own(z, t, h)]
                    for k in range(3):
                        source = ec if n == steps - 1 else vb
                        new = source[(k,) + own(z, t, h)] - div[h][k]
                        target = vb if n > 0 else out_ref
                        target[(k,) + own(z, t, h)] = new
                        vs[slot, k, tile.at(h), :] = b * new
            return carry

        lax.fori_loop(0, NZ_OWN, body, 0)

    corner_fields = ((0, 2), (0, 1), (1, 2), (0, 1, 2))

    def send_velocity(p):
        v = vs.at[p]
        wide = p < 2 * steps - 1
        to_low, to_high = (WIDE_LOW, WIDE_HIGH) if wide else (THIN_LOW, THIN_HIGH)
        step = Exchange()

        def layers(field, count, z, depth):
            return v.at[pl.ds(field, count), pl.ds(row_of(z, 0), depth * LAYER), :]

        if wide:
            step.depth = [
                remote(layers(0, 2, last, 1), layers(0, 2, -1, 1), (down, l)),
                remote(layers(2, 1, last - 1, 2), layers(2, 1, -2, 2), (down, l)),
                remote(layers(0, 2, 0, 2), layers(0, 2, NZ_OWN, 2), (up, l)),
                remote(layers(2, 1, 0, 1), layers(2, 1, NZ_OWN, 1), (up, l)),
            ]
        else:
            step.depth = [
                remote(layers(2, 1, last, 1), layers(2, 1, -1, 1), (down, l)),
                remote(layers(0, 2, 0, 1), layers(0, 2, NZ_OWN, 1), (up, l)),
            ]
        for k, (field, here, there) in enumerate(to_low):
            for h in range(2):
                vx_send[p, 0, 2 * k + h] = face(v, field, here, h)
        for k, (field, here, there) in enumerate(to_high):
            for h in range(2):
                vx_send[p, 1, 2 * k + h] = face(v, field, here, h)
        if wide:
            for c, (x, z) in enumerate(((15, last), (15, 0), (0, last), (0, 0))):
                for field in corner_fields[c]:
                    for h in range(2):
                        cor_send[p, c, pl.ds(2 * field + h, 1), :] = v[field, pl.ds(row_of(z, x, h), 1), :]
            step.high = [
                remote(cor_send.at[p, 0], cor_recv.at[p, 0], (down, high)),
                remote(cor_send.at[p, 1], cor_recv.at[p, 1], (up, high)),
            ]
            step.low = [
                remote(cor_send.at[p, 2], cor_recv.at[p, 2], (down, low)),
                remote(cor_send.at[p, 3], cor_recv.at[p, 3], (up, low)),
            ]
        count = 2 * len(to_low)
        step.low.append(remote(vx_send.at[p, 0, pl.ds(0, count)], vx_high.at[p, pl.ds(0, count)], (d, low)))
        count = 2 * len(to_high)
        step.high.append(remote(vx_send.at[p, 1, pl.ds(0, count)], vx_low.at[p, pl.ds(0, count)], (d, high)))
        step.start()
        return step

    def take_velocity(p, step):
        v = vs.at[p]
        wide = p < 2 * steps - 1
        to_low, to_high = (WIDE_LOW, WIDE_HIGH) if wide else (THIN_LOW, THIN_HIGH)
        step.wait_send()
        step.wait_recv()

        def clear(field, z, depth):
            def body(i, carry):
                v[field, pl.ds(row_of(z, 0) + 8 * i, 8), :] = zero
                return carry

            lax.fori_loop(0, depth * LAYER // 8, body, 0)

        @pl.when(top)
        def _():
            if wide:
                clear(0, -1, 1)
                clear(1, -1, 1)
                clear(2, -2, 2)
            else:
                clear(2, -1, 1)

        @pl.when(bottom)
        def _():
            for field in range(2):
                clear(field, NZ_OWN, 2 if wide else 1)
            if wide:
                clear(2, NZ_OWN, 1)

        for k, (field, here, there) in enumerate(to_low):
            for h in range(2):
                put_face(v, field, there, h, vx_high[p, 2 * k + h])
        for k, (field, here, there) in enumerate(to_high):
            for h in range(2):
                put_face(v, field, there, h, vx_low[p, 2 * k + h])
        if wide:
            for c, (x, z, outside) in enumerate(
                ((-1, -1, top), (-1, NZ_OWN, bottom), (NX_OWN, -1, top), (NX_OWN, NZ_OWN, bottom))
            ):
                for field in corner_fields[c]:
                    for h in range(2):
                        value = cor_recv[p, c, pl.ds(2 * field + h, 1), :]
                        v[field, pl.ds(row_of(z, x, h), 1), :] = jnp.where(outside, 0.0, value)

    rounds = []
    reach = 2
    while reach < nd // 2:
        rounds.append(reach)
        reach *= 2

    def far_signal(i):
        if i < len(rounds):
            for way, other in enumerate((lax.rem(d + rounds[i], nd), lax.rem(d + nd - rounds[i], nd))):
                pl.semaphore_signal(far_sem.at[2 * i + way], inc=1, device_id=(other, l), device_id_type=MESH)

    def far_wait(i):
        if i < len(rounds):
            for way in range(2):
                pl.semaphore_wait(far_sem.at[2 * i + way], 1)

    def note_surface(gain, w_slot, start):
        @pl.when(top)
        def _():
            for t in range(2):
                for h in range(2):
                    place = pl.ds(row_of(0, 8 * t, h), 8)
                    if w_slot is None:
                        value = sp[2, place, :]
                    else:
                        value = sp[2, place, :] - vs[w_slot, 2, place, :]
                    spot = pl.ds(16 * h + 8 * t, 8)
                    q_map[spot, :] = gain * value if start else q_map[spot, :] + gain * value

    y_copies = [remote(psum_buf.at[0], ysum_buf.at[l_y], (d, peer)) for peer in y_peers]
    x_copies = [remote(psum_buf.at[1], xsum_buf.at[l_x], (d, peer)) for peer in x_peers]

    def add_up_pulses():
        @pl.when(top)
        def _():
            bins = lax.broadcasted_iota(jnp.int32, (pulses, 128), 0)
            total = jnp.zeros((pulses, 128), F32)
            for t in range(2):
                for h in range(2):
                    foot = fp_ref[pl.ds(8 * t, 8), pl.ds(128 * h, 128)]
                    value = q_map[pl.ds(16 * h + 8 * t, 8), :]
                    for i in range(8):
                        total = total + jnp.where(
                            jnp.broadcast_to(foot[i : i + 1], (pulses, 128)) == bins,
                            jnp.broadcast_to(value[i : i + 1], (pulses, 128)),
                            0.0,
                        )
            sums = lax.dot_general(
                jnp.ones((8, 128), F32), total, (((1,), (1,)), ((), ())),
                precision=lax.Precision.HIGHEST, preferred_element_type=F32,
            )
            psum_buf[0] = zero
            psum_buf[0, :, pl.ds(0, pulses)] = sums
            for copy in y_copies:
                copy.start()
            ysum_buf[l_y] = psum_buf[0]
            for copy in y_copies:
                copy.wait_recv()
            sums = ysum_buf[0]
            for k in range(1, wide_y):
                sums = sums + ysum_buf[k]
            psum_buf[1] = sums
            for copy in x_copies:
                copy.start()
            xsum_buf[l_x] = sums
            for copy in y_copies:
                copy.wait_send()

    chips = nd // 2
    far = sorted(range(1, chips), key=lambda k: -min(k, chips - k))
    far_ids = [next(ids) for _ in far]
    core_id = next(ids)

    def spread_copy(k, send_id):
        return pltpu.make_async_remote_copy(
            src_ref=total_buf, dst_ref=total_buf, send_sem=send_sem.at[send_id], recv_sem=recv_sem.at[far_ids[0]],
            device_id=(2 * k, l), device_id_type=MESH,
        )

    core_copy = pltpu.make_async_remote_copy(
        src_ref=total_buf, dst_ref=total_buf, send_sem=send_sem.at[core_id], recv_sem=recv_sem.at[core_id],
        device_id=(d + 1 - 2 * lax.rem(d, 2), l), device_id_type=MESH,
    )
    scale = math.sqrt(pulses / (NX_OWN * nl * 256))

    def spread_pulses():
        @pl.when(top)
        def _():
            for copy in x_copies:
                copy.wait_recv()
            sums = xsum_buf[0]
            for k in range(1, n_x):
                sums = sums + xsum_buf[k]
            total_buf[...] = sums * scale
            for k, send_id in zip(far, far_ids):
                spread_copy(k, send_id).start()
            core_copy.start()
            for copy in x_copies:
                copy.wait_send()

    def finish_pulses():
        even = lax.rem(d, 2) == 0

        @pl.when(jnp.logical_and(even, jnp.logical_not(top)))
        def _():
            spread_copy(1, far_ids[0]).wait_recv()
            core_copy.start()

        @pl.when(jnp.logical_not(even))
        def _():
            core_copy.wait_recv()

        pulse_ref[...] = total_buf[...]

        @pl.when(even)
        def _():
            core_copy.wait_send()

        @pl.when(top)
        def _():
            for k, send_id in zip(far, far_ids):
                spread_copy(k, send_id).wait_send()

    note_surface(gains[steps - 1], None, True)
    first_faces.wait_recv()
    put_stress(((4, 5), (2,), (3, 4), (0,)))
    forward_velocity(0)
    step = send_velocity(0)
    far_signal(0)
    rest.wait_recv()
    put_stress(((0, 1, 2, 3), (0, 1, 3, 4, 5), (0, 1, 2, 5), (1, 2, 3, 4, 5)))
    for k in range(3):
        put_layer(cf, k, -1, zc_low.at[k], None)
        put_layer(cf, k, NZ_OWN, zc_high.at[k], None)
        put_layer(cf, 3 + k, -1, zm_low.at[k], None)
        put_layer(cf, 3 + k, NZ_OWN, zm_high.at[k], None)
    for k in range(6):
        for h in range(2):
            put_face(cf, k, -1, h, fx_low[12 + 2 * k + h])
            put_face(cf, k, NX_OWN, h, fx_high[12 + 2 * k + h])
    for h in range(2):
        load_map[pl.ds(BASE + GROUP * h - 1, 1), :] = fx_low[24, pl.ds(h, 1), :]
        load_map[pl.ds(BASE + GROUP * h + NX_OWN, 1), :] = fx_high[24, pl.ds(h, 1), :]
    for n in range(steps - 1):
        take_velocity(n, step)
        far_wait(n)
        forward_stress(n)
        forward_velocity(n + 1)
        step = send_velocity(n + 1)
        far_signal(n + 1)
        if n == 0:
            ends.wait_recv()
            for k in range(6):
                put_layer(sp, k, -1, zs_low.at[6 + k], None)
                put_layer(sp, k, NZ_OWN, zs_high.at[6 + k], None)
                for h in range(2):
                    put_face(sp, k, -1, h, fx_low[25 + 2 * k + h])
                    put_face(sp, k, NX_OWN, h, fx_high[25 + 2 * k + h])

    take_velocity(steps - 1, step)
    far_wait(steps - 1)
    turn()
    pulse_sends = []
    for n in range(steps - 1, -1, -1):
        backward_velocity(n)
        slot = 2 * steps - 1 - n
        step = send_velocity(slot)
        if n == 0:
            spread_pulses()
        if n > 0:
            note_surface(gains[n - 1], slot, False)
        if n == 1:
            add_up_pulses()
        take_velocity(slot, step)
        if n > 0:
            backward_stress(n - 1)

    def last_stress(z, carry):
        for t in range(2):
            tile = Tile(row_of(z, 8 * t))
            back = gradient(tile, vs.at[2 * steps - 1])
            for h in range(2):
                for k in range(6):
                    out_ref[(3 + k,) + own(z, t, h)] = sp[k, tile.at(h), :] - back[h][k]
        return carry

    lax.fori_loop(0, NZ_OWN, last_stress, 0)
    finish_pulses()
    for exchange in (first_faces, rest, ends):
        exchange.wait_send()


def per_device(mesh_shape, checkpoint, end_cotangent, buoyancy, moduli, yield_radius, mask, footprint, amplitude):
    steps = mask.shape[0]
    pulses = amplitude.shape[0]
    nd, nl = mesh_shape
    phases = 2 * steps
    vmem = pltpu.VMEM
    ext = (ROWS, 128)
    tile = (8, 128)
    anywhere = pl.BlockSpec(memory_space=pl.ANY)
    in_vmem = pl.BlockSpec(memory_space=pltpu.VMEM)
    scratch = [vmem(a.shape, a.dtype) for a in (checkpoint, end_cotangent, buoyancy, moduli, yield_radius, mask)]
    plane = checkpoint.shape[2:]
    scratch += [
        vmem((6,) + ext, F32),
        vmem((6,) + ext, F32),
        vmem((6,) + ext, F32),
        vmem((phases, 3) + ext, F32),
        vmem((3,) + buoyancy.shape, F32),
        vmem((steps - 1, 8) + ext, F32),
        vmem((3 + steps,) + ext, F32),
        vmem((64, 128), F32),
        vmem((32, 128), F32),
        vmem((2, 37) + tile, F32),
        vmem((37,) + tile, F32),
        vmem((37,) + tile, F32),
        vmem((12,) + plane, F32),
        vmem((12,) + plane, F32),
        vmem((3,) + plane, F32),
        vmem((3,) + plane, F32),
        vmem((steps,) + plane, jnp.int32),
        vmem((steps,) + plane, jnp.int32),
        vmem((phases, 2, 10) + tile, F32),
        vmem((phases, 10) + tile, F32),
        vmem((phases, 10) + tile, F32),
        vmem((phases - 1, 4) + tile, F32),
        vmem((phases - 1, 4) + tile, F32),
        vmem((2,) + tile, F32),
        vmem((4,) + tile, F32),
        vmem((4,) + tile, F32),
        vmem(tile, F32),
        pltpu.SemaphoreType.DMA((6,)),
        pltpu.SemaphoreType.DMA((112,)),
        pltpu.SemaphoreType.DMA((112,)),
        pltpu.SemaphoreType.REGULAR((8,)),
    ]
    adjoint, sums = pl.pallas_call(
        functools.partial(kernel, nd, nl, steps, pulses, 4),
        out_shape=(
            jax.ShapeDtypeStruct(checkpoint.shape, F32),
            jax.ShapeDtypeStruct(tile, F32),
        ),
        in_specs=[anywhere] * 6 + [in_vmem, pl.BlockSpec(memory_space=pltpu.SMEM)],
        out_specs=(in_vmem, in_vmem),
        scratch_shapes=scratch,
        compiler_params=pltpu.CompilerParams(
            collective_id=0, has_side_effects=True, vmem_limit_bytes=48 * 2**20
        ),
    )(checkpoint, end_cotangent, buoyancy, moduli, yield_radius, mask, footprint, amplitude)
    return adjoint, sums[0, :pulses]


def solution(mesh):
    placed = (
        P(None, "depth", "lat", None),
        P(None, "depth", "lat", None),
        P("depth", "lat", None),
        P(None, "depth", "lat", None),
        P("depth", "lat", None),
        P(None, "depth", "lat", None),
        P("lat", None),
        P(),
    )
    return jax.shard_map(
        functools.partial(per_device, (mesh.shape["depth"], mesh.shape["lat"])),
        mesh=mesh,
        in_specs=placed,
        out_specs=(P(None, "depth", "lat", None), P()),
        check_vma=False,
    )
```

```python
import functools
import math

import jax
import jax.numpy as jnp
from jax import lax
from jax.experimental import pallas as pl
from jax.experimental.pallas import tpu as pltpu
from jax.sharding import PartitionSpec as P

MESH = pl.DeviceIdType.MESH
F32 = jnp.float32

NZ_OWN = 8
NX_OWN = 16
GROUP = 24
LAYER = 2 * GROUP
BASE = 8
UNROLL_S = 2
UNROLL_V = 8
UNROLL_H = 2
ROWS = BASE + (NZ_OWN + 4) * LAYER


def row_of(z, x, half=0):
    return BASE + LAYER * (z + 2) + GROUP * half + x


class Tile:
    def __init__(self, row, stride=1):
        self.row = row
        self.stride = stride

    def at(self, half, shift=0):
        start = self.row + GROUP * half + shift
        return pl.ds(start, 8) if self.stride == 1 else pl.ds(start, 8, self.stride)

    def load(self, ref, field, dz=0, dx=0):
        return [ref[field, self.at(half, LAYER * dz + dx), :] for half in range(2)]

    def store(self, later, ref, field, half, value):
        later.append((ref, field, self.at(half), value))


def y_shifts():
    lane = lax.broadcasted_iota(jnp.int32, (8, 128), 1)
    first = lane == 0
    last = lane == 127

    def before(pair):
        low, high = pltpu.roll(pair[0], 1, 1), pltpu.roll(pair[1], 1, 1)
        return [jnp.where(first, 0.0, low), jnp.where(first, low, high)]

    def after(pair):
        low, high = pltpu.roll(pair[0], 127, 1), pltpu.roll(pair[1], 127, 1)
        return [jnp.where(last, high, low), jnp.where(last, 0.0, high)]

    return before, after


def divergence(tile, ref):
    before, after = y_shifts()
    c = [tile.load(ref, k) for k in range(6)]
    xx_next = tile.load(ref, 0, dx=1)
    xy_prev = tile.load(ref, 3, dx=-1)
    xz_prev = tile.load(ref, 4, dx=-1)
    xz_up = tile.load(ref, 4, dz=-1)
    yz_up = tile.load(ref, 5, dz=-1)
    zz_down = tile.load(ref, 2, dz=1)
    xy_y = before(c[3])
    yz_y = before(c[5])
    yy_y = after(c[1])
    out = []
    for h in range(2):
        out.append(
            (
                (xx_next[h] - c[0][h]) + (c[3][h] - xy_y[h]) + (c[4][h] - xz_up[h]),
                (c[3][h] - xy_prev[h]) + (yy_y[h] - c[1][h]) + (c[5][h] - yz_up[h]),
                (c[4][h] - xz_prev[h]) + (c[5][h] - yz_y[h]) + (zz_down[h] - c[2][h]),
            )
        )
    return out


def y_differences(w):
    before, after = y_shifts()
    wy_y, wx_y, wz_y = before(w[1]), after(w[0]), after(w[2])
    return (
        [w[1][h] - wy_y[h] for h in range(2)],
        [wx_y[h] - w[0][h] for h in range(2)],
        [wz_y[h] - w[2][h] for h in range(2)],
    )


def gradient(tile, ref, along_y=None):
    w = [tile.load(ref, k) for k in range(3)]
    gy = y_differences(w) if along_y is None else [tile.load(along_y, k) for k in range(3)]
    wx_prev = tile.load(ref, 0, dx=-1)
    wz_up = tile.load(ref, 2, dz=-1)
    wy_next = tile.load(ref, 1, dx=1)
    wz_next = tile.load(ref, 2, dx=1)
    wx_down = tile.load(ref, 0, dz=1)
    wy_down = tile.load(ref, 1, dz=1)
    out = []
    for h in range(2):
        out.append(
            (
                w[0][h] - wx_prev[h],
                gy[0][h],
                w[2][h] - wz_up[h],
                gy[1][h] + (wy_next[h] - w[1][h]),
                (wx_down[h] - w[0][h]) + (wz_next[h] - w[2][h]),
                (wy_down[h] - w[1][h]) + gy[2][h],
            )
        )
    return out


def trial(s, e, lame, shear, limit, plastic):
    volume = lame * (e[0] + e[1] + e[2])
    twice = 2.0 * shear
    normal = [s[a] + volume + twice * e[a] for a in range(3)]
    shears = [s[a] + shear * e[a] for a in range(3, 6)]
    mean = (normal[0] + normal[1] + normal[2]) * (1.0 / 3.0)
    devs = [normal[a] - mean for a in range(3)]
    qsq = (devs[0] * devs[0] + devs[1] * devs[1] + devs[2] * devs[2]) + 2.0 * (
        shears[0] * shears[0] + shears[1] * shears[1] + shears[2] * shears[2]
    )
    inverse = lax.rsqrt(limit * limit + qsq)
    scaled = plastic * limit * inverse
    factor = (1.0 - plastic) + scaled
    slope = scaled * (inverse * inverse)
    return mean, devs + shears, factor, slope


def pull_back(g, parts, factor, slope, lame, shear):
    along = (g[0] * parts[0] + g[1] * parts[1] + g[2] * parts[2]) + (
        g[3] * parts[3] + g[4] * parts[4] + g[5] * parts[5]
    )
    pull = slope * along
    pull_twice = pull + pull
    total = g[0] + g[1] + g[2]
    rest = (1.0 - factor) * (total * (1.0 / 3.0))
    twice = 2.0 * shear
    volume = lame * total
    stress = [factor * g[a] - pull * parts[a] + rest for a in range(3)]
    stress += [factor * g[a] - pull_twice * parts[a] for a in range(3, 6)]
    strain = [volume + twice * stress[a] for a in range(3)]
    strain += [shear * stress[a] for a in range(3, 6)]
    return stress, strain


TO_LOW = (0, 1, 2, 3, 4, 5)
TO_HIGH = (3, 4, 0, 1, 2, 5)
WIDE_LOW = ((0, 0, 16), (1, 0, 16), (2, 0, 16), (1, 1, 17), (2, 1, 17))
WIDE_HIGH = ((0, 15, -1), (1, 15, -1), (2, 15, -1), (0, 14, -2))
THIN_LOW = ((1, 0, 16), (2, 0, 16))
THIN_HIGH = ((0, 15, -1),)


def kernel(
    nd, nl, steps, pulses, wide_y,
    cp_in, ec_in, bu_in, mo_in, yi_in, ma_in, fp_in, amp_in,
    out_ref, pulse_ref,
    cp, ec, bu, mo, yi, ma, fp_ref, amp_ref,
    st, sp, co, vs, vb, hist, cf, gy,
    load_map, q_map, fx_send, fx_low, fx_high, zs_low, zs_high, zc_low, zc_high, zm_low, zm_high,
    vx_send, vx_low, vx_high, cor_send, cor_recv,
    psum_buf, ysum_buf, xsum_buf, total_buf,
    in_sem, send_sem, recv_sem, far_sem,
):
    d = lax.axis_index("depth")
    l = lax.axis_index("lat")
    top = d == 0
    bottom = d == nd - 1
    has_low = l > 0
    has_high = l < nl - 1
    up = lax.rem(d + nd - 1, nd)
    down = lax.rem(d + 1, nd)
    low = jnp.maximum(l - 1, 0)
    high = jnp.minimum(l + 1, nl - 1)
    gains = [math.sin(math.pi * (n + 0.5) / steps) for n in range(steps)]

    def load_in(k, source, target):
        copy = pltpu.make_async_copy(source, target, in_sem.at[k])
        copy.start()
        return copy

    stress_in = load_in(0, cp_in.at[pl.ds(3, 6)], cp.at[pl.ds(3, 6)])

    barrier = pltpu.get_barrier_semaphore()

    def greet(dd, ll):
        pl.semaphore_signal(barrier, inc=1, device_id=(dd, ll), device_id_type=MESH)

    greet(up, l)
    greet(down, l)

    @pl.when(has_low)
    def _():
        greet(d, low)
        greet(up, low)
        greet(down, low)

    @pl.when(has_high)
    def _():
        greet(d, high)
        greet(up, high)
        greet(down, high)

    l_y = lax.rem(l, wide_y)
    l_x = l // wide_y
    n_x = nl // wide_y
    y_peers = [l_x * wide_y + lax.rem(l_y + k, wide_y) for k in range(1, wide_y)]
    x_peers = [lax.rem(l_x + k, n_x) * wide_y + l_y for k in range(1, n_x)]

    @pl.when(top)
    def _():
        for peer in y_peers + x_peers:
            greet(d, peer)

    others = ((mo_in, mo), (yi_in, yi), (ma_in, ma), (fp_in, fp_ref), (amp_in, amp_ref), (bu_in, bu), (ec_in, ec))
    static_in = [load_in(1 + k, source, target) for k, (source, target) in enumerate(others[:5])]
    velocity_in = load_in(6, cp_in.at[pl.ds(0, 3)], cp.at[pl.ds(0, 3)])
    late_in = [load_in(7 + k, source, target) for k, (source, target) in enumerate(others[5:])]
    ids = iter(range(1000))

    def remote(source, target, where):
        k = next(ids)
        return pltpu.make_async_remote_copy(
            src_ref=source, dst_ref=target, send_sem=send_sem.at[k], recv_sem=recv_sem.at[k],
            device_id=where, device_id_type=MESH,
        )

    def own(z, t, h):
        return (z, pl.ds(8 * t, 8), pl.ds(128 * h, 128))

    def stage_stress(z, carry):
        for t in range(2):
            for h in range(2):
                for k in range(6):
                    st[k, pl.ds(row_of(z, 8 * t, h), 8), :] = cp[(3 + k,) + own(z, t, h)]
        return carry

    def face(ref, field, x, h):
        return ref[field, pl.ds(row_of(0, x, h), NZ_OWN, LAYER), :]

    stress_in.wait()
    lax.fori_loop(0, NZ_OWN, stage_stress, 0)
    for side, order, x, count in ((0, TO_LOW, 0, 1), (1, TO_HIGH, NX_OWN - 1, 2)):
        for k in range(count):
            for h in range(2):
                fx_send[side, 2 * k + h] = face(st, order[k], x, h)

    near = 2 + 3 * has_low.astype(jnp.int32) + 3 * has_high.astype(jnp.int32)
    pl.semaphore_wait(barrier, near + top.astype(jnp.int32) * (len(y_peers) + len(x_peers)))

    class Exchange:
        def __init__(self):
            self.depth, self.low, self.high = [], [], []

        def start(self):
            @pl.when(has_low)
            def _():
                for copy in self.low:
                    copy.start()

            @pl.when(has_high)
            def _():
                for copy in self.high:
                    copy.start()

            for copy in self.depth:
                copy.start()

        def wait_send(self):
            for copy in self.depth:
                copy.wait_send()

            @pl.when(has_low)
            def _():
                for copy in self.low:
                    copy.wait_send()

            @pl.when(has_high)
            def _():
                for copy in self.high:
                    copy.wait_send()

        def wait_recv(self):
            for copy in self.depth:
                copy.wait_recv()

            @pl.when(has_high)
            def _():
                for copy in self.low:
                    copy.wait_recv()

            @pl.when(has_low)
            def _():
                for copy in self.high:
                    copy.wait_recv()

    last = NZ_OWN - 1
    first_faces = Exchange()
    first_faces.depth = [
        remote(cp.at[pl.ds(7, 2), last], zs_low.at[pl.ds(4, 2)], (down, l)),
        remote(cp.at[pl.ds(5, 1), 0], zs_high.at[pl.ds(2, 1)], (up, l)),
    ]
    first_faces.low = [remote(fx_send.at[0, pl.ds(0, 2)], fx_high.at[pl.ds(0, 2)], (d, low))]
    first_faces.high = [remote(fx_send.at[1, pl.ds(0, 4)], fx_low.at[pl.ds(0, 4)], (d, high))]
    first_faces.start()
    def stage(z, carry):
        for t in range(2):
            for h in range(2):
                place = pl.ds(row_of(z, 8 * t, h), 8)
                cf[0, place, :] = mo[(0,) + own(z, t, h)]
                cf[1, place, :] = mo[(1,) + own(z, t, h)]
                cf[2, place, :] = yi[own(z, t, h)]
                for k in range(3):
                    cf[3 + k, place, :] = ma[(k,) + own(z, t, h)].astype(F32)
        return carry

    def stage_end(z, carry):
        for t in range(2):
            for h in range(2):
                place = pl.ds(row_of(z, 8 * t, h), 8)
                for k in range(6):
                    sp[k, place, :] = ec[(3 + k,) + own(z, t, h)]
        return carry

    for copy in static_in:
        copy.wait()
    lax.fori_loop(0, NZ_OWN, stage, 0)

    load_map[...] = jnp.zeros_like(load_map)

    @pl.when(top)
    def _():
        for t in range(2):
            for h in range(2):
                foot = fp_ref[pl.ds(8 * t, 8), pl.ds(128 * h, 128)]

                def add(p, total, foot=foot):
                    return jnp.where(foot == p, amp_ref[p], total)

                load_map[pl.ds(BASE + GROUP * h + 8 * t, 8), :] = lax.fori_loop(
                    0, pulses, add, jnp.zeros((8, 128), F32), unroll=8
                )

    zero = jnp.zeros((8, 128), F32)

    @pl.when(jnp.logical_not(has_low))
    def _():
        fx_low[...] = jnp.zeros_like(fx_low)
        vx_low[...] = jnp.zeros_like(vx_low)
        for p in range(2 * steps - 1):
            cor_recv[p, 0] = zero
            cor_recv[p, 1] = zero

    @pl.when(jnp.logical_not(has_high))
    def _():
        fx_high[...] = jnp.zeros_like(fx_high)
        vx_high[...] = jnp.zeros_like(vx_high)
        for p in range(2 * steps - 1):
            cor_recv[p, 2] = zero
            cor_recv[p, 3] = zero

    for side, order, x, count in ((0, TO_LOW, 0, 1), (1, TO_HIGH, NX_OWN - 1, 2)):
        for k in range(count, 6):
            for h in range(2):
                fx_send[side, 2 * k + h] = face(st, order[k], x, h)
        for k in range(6):
            for h in range(2):
                fx_send[side, 12 + 2 * k + h] = face(cf, k, x, h)
        for h in range(2):
            fx_send[side, 24, pl.ds(h, 1), :] = load_map[pl.ds(BASE + GROUP * h + x, 1), :]

    rest = Exchange()
    rest.depth = [
        remote(cp.at[pl.ds(3, 4), last], zs_low.at[pl.ds(0, 4)], (down, l)),
        remote(mo.at[:, last], zc_low.at[pl.ds(0, 2)], (down, l)),
        remote(yi.at[pl.ds(last, 1)], zc_low.at[pl.ds(2, 1)], (down, l)),
        remote(ma.at[:, last], zm_low, (down, l)),
        remote(cp.at[pl.ds(3, 2), 0], zs_high.at[pl.ds(0, 2)], (up, l)),
        remote(cp.at[pl.ds(6, 3), 0], zs_high.at[pl.ds(3, 3)], (up, l)),
        remote(mo.at[:, 0], zc_high.at[pl.ds(0, 2)], (up, l)),
        remote(yi.at[pl.ds(0, 1)], zc_high.at[pl.ds(2, 1)], (up, l)),
        remote(ma.at[:, 0], zm_high, (up, l)),
    ]
    rest.low = [remote(fx_send.at[0, pl.ds(2, 23)], fx_high.at[pl.ds(2, 23)], (d, low))]
    rest.high = [remote(fx_send.at[1, pl.ds(4, 21)], fx_low.at[pl.ds(4, 21)], (d, high))]
    rest.start()

    velocity_in.wait()
    for copy in late_in:
        copy.wait()
    lax.fori_loop(0, NZ_OWN, stage_end, 0)
    for side, x in ((0, 0), (1, NX_OWN - 1)):
        for k in range(6):
            for h in range(2):
                fx_send[side, 25 + 2 * k + h] = face(sp, k, x, h)
    ends = Exchange()
    ends.depth = [
        remote(ec.at[pl.ds(3, 6), last], zs_low.at[pl.ds(6, 6)], (down, l)),
        remote(ec.at[pl.ds(3, 6), 0], zs_high.at[pl.ds(6, 6)], (up, l)),
    ]
    ends.low = [remote(fx_send.at[0, pl.ds(25, 12)], fx_high.at[pl.ds(25, 12)], (d, low))]
    ends.high = [remote(fx_send.at[1, pl.ds(25, 12)], fx_low.at[pl.ds(25, 12)], (d, high))]
    ends.start()

    def put_face(ref, field, x, h, value):
        ref[field, pl.ds(row_of(0, x, h), NZ_OWN, LAYER), :] = value

    def put_layer(ref, field, z, source, outside):
        for t in range(2):
            for h in range(2):
                value = source[pl.ds(8 * t, 8), pl.ds(128 * h, 128)].astype(F32)
                if outside is not None:
                    value = jnp.where(outside, 0.0, value)
                ref[field, pl.ds(row_of(z, 8 * t, h), 8), :] = value

    def put_stress(fields):
        for field in fields[0]:
            put_layer(st, field, -1, zs_low.at[field], top)
        for field in fields[1]:
            put_layer(st, field, NZ_OWN, zs_high.at[field], bottom)
        for field in fields[2]:
            for h in range(2):
                put_face(st, field, -1, h, fx_low[2 * TO_HIGH.index(field) + h])
        for field in fields[3]:
            for h in range(2):
                put_face(st, field, NX_OWN, h, fx_high[2 * TO_LOW.index(field) + h])

    inside_z = [jnp.logical_not(top), jnp.logical_not(bottom)]

    def write(later):
        for ref, field, place, value in later:
            ref[field, place, :] = value

    def everywhere(unit):
        def inner(z, carry):
            later = []
            for t in range(2):
                unit(later, Tile(row_of(z, 8 * t)), None, gy)
            write(later)
            return carry

        lax.fori_loop(0, NZ_OWN, inner, 0, unroll=UNROLL_S)

        def outer(side, carry):
            z = -1 + (NZ_OWN + 1) * side
            inside = jnp.where(side == 0, inside_z[0].astype(jnp.int32), inside_z[1].astype(jnp.int32)) > 0
            later = []
            for t in range(2):
                unit(later, Tile(row_of(z, 8 * t)), inside, None)
            write(later)
            return carry

        lax.fori_loop(0, 2, outer, 0, unroll=UNROLL_H)
        later = []
        unit(later, Tile(row_of(0, -1), LAYER), has_low, None)
        unit(later, Tile(row_of(0, NX_OWN), LAYER), has_high, None)
        write(later)

    def keep(inside, value):
        return value if inside is None else jnp.where(inside, value, 0.0)

    def coefficients(tile, n):
        return [tile.load(cf, k) for k in (0, 1, 2, 3 + n)]

    def forward_stress(n):
        v = vs.at[n]
        record = hist.at[n]

        def unit(later, tile, inside, along_y):
            e = gradient(tile, v, along_y)
            s = [tile.load(st, k) for k in range(6)]
            lame, shear, limit, plastic = coefficients(tile, n)
            for h in range(2):
                mean, parts, factor, slope = trial(
                    [s[k][h] for k in range(6)], e[h], lame[h], shear[h], limit[h], plastic[h]
                )
                for k in range(6):
                    value = factor * parts[k]
                    if k < 3:
                        value = mean + value
                    tile.store(later, st, k, h, keep(inside, value))
                    tile.store(later, record, k, h, parts[k])
                tile.store(later, record, 6, h, factor)
                tile.store(later, record, 7, h, slope)

        everywhere(unit)

        @pl.when(top)
        def _():
            for h in range(2):
                for x, count in ((-1, 1), (0, 8), (8, 8), (16, 1)):
                    place = pl.ds(row_of(0, x, h), count)
                    st[2, place, :] += gains[n] * load_map[pl.ds(BASE + GROUP * h + x, count), :]

    def turn():
        n = steps - 1
        v = vs.at[n]

        def unit(later, tile, inside, along_y):
            e = gradient(tile, v, along_y)
            s = [tile.load(st, k) for k in range(6)]
            g = [tile.load(sp, k) for k in range(6)]
            lame, shear, limit, plastic = coefficients(tile, n)
            for h in range(2):
                mean, parts, factor, slope = trial(
                    [s[k][h] for k in range(6)], e[h], lame[h], shear[h], limit[h], plastic[h]
                )
                stress, strain = pull_back([g[k][h] for k in range(6)], parts, factor, slope, lame[h], shear[h])
                for k in range(6):
                    tile.store(later, sp, k, h, stress[k])
                    tile.store(later, co, k, h, keep(inside, strain[k]))

        everywhere(unit)

    def backward_stress(n):
        w = vs.at[2 * steps - 2 - n]
        record = hist.at[n]

        def unit(later, tile, inside, along_y):
            back = gradient(tile, w, along_y)
            s = [tile.load(sp, k) for k in range(6)]
            kept = [tile.load(record, k) for k in range(8)]
            lame, shear = tile.load(cf, 0), tile.load(cf, 1)
            for h in range(2):
                g = [s[k][h] - back[h][k] for k in range(6)]
                stress, strain = pull_back(
                    g, [kept[k][h] for k in range(6)], kept[6][h], kept[7][h], lame[h], shear[h]
                )
                for k in range(6):
                    tile.store(later, sp, k, h, stress[k])
                    tile.store(later, co, k, h, keep(inside, strain[k]))

        everywhere(unit)

    def forward_velocity(n):
        def body(z, carry):
            later = []
            for t in range(2):
                tile = Tile(row_of(z, 8 * t))
                div = divergence(tile, st)
                for h in range(2):
                    b = bu[own(z, t, h)]
                    for k in range(3):
                        old = cp[(k,) + own(z, t, h)] if n == 0 else vs[n - 1, k, tile.at(h), :]
                        tile.store(later, vs.at[n], k, h, old + b * div[h][k])
            write(later)
            return carry

        lax.fori_loop(0, NZ_OWN, body, 0, unroll=UNROLL_V)

    def backward_velocity(n):
        slot = 2 * steps - 1 - n

        def body(z, carry):
            later = []
            plain = []
            for t in range(2):
                tile = Tile(row_of(z, 8 * t))
                div = divergence(tile, co)
                for h in range(2):
                    b = bu[own(z, t, h)]
                    for k in range(3):
                        source = ec if n == steps - 1 else vb
                        new = source[(k,) + own(z, t, h)] - div[h][k]
                        plain.append(((k,) + own(z, t, h), new))
                        tile.store(later, vs.at[slot], k, h, b * new)
            for place, new in plain:
                target = vb if n > 0 else out_ref
                target[place] = new
            write(later)
            return carry

        lax.fori_loop(0, NZ_OWN, body, 0, unroll=UNROLL_V)

    corner_fields = ((0, 2), (0, 1), (1, 2), (0, 1, 2))

    def send_velocity(p):
        v = vs.at[p]
        wide = p < 2 * steps - 1
        to_low, to_high = (WIDE_LOW, WIDE_HIGH) if wide else (THIN_LOW, THIN_HIGH)
        step = Exchange()

        def layers(field, count, z, depth):
            return v.at[pl.ds(field, count), pl.ds(row_of(z, 0), depth * LAYER), :]

        if wide:
            step.depth = [
                remote(layers(0, 2, last, 1), layers(0, 2, -1, 1), (down, l)),
                remote(layers(2, 1, last - 1, 2), layers(2, 1, -2, 2), (down, l)),
                remote(layers(0, 2, 0, 2), layers(0, 2, NZ_OWN, 2), (up, l)),
                remote(layers(2, 1, 0, 1), layers(2, 1, NZ_OWN, 1), (up, l)),
            ]
        else:
            step.depth = [
                remote(layers(2, 1, last, 1), layers(2, 1, -1, 1), (down, l)),
                remote(layers(0, 2, 0, 1), layers(0, 2, NZ_OWN, 1), (up, l)),
            ]
        for k, (field, here, there) in enumerate(to_low):
            for h in range(2):
                vx_send[p, 0, 2 * k + h] = face(v, field, here, h)
        for k, (field, here, there) in enumerate(to_high):
            for h in range(2):
                vx_send[p, 1, 2 * k + h] = face(v, field, here, h)
        if wide:
            for c, (x, z) in enumerate(((15, last), (15, 0), (0, last), (0, 0))):
                for field in corner_fields[c]:
                    for h in range(2):
                        cor_send[p, c, pl.ds(2 * field + h, 1), :] = v[field, pl.ds(row_of(z, x, h), 1), :]
            step.high = [
                remote(cor_send.at[p, 0], cor_recv.at[p, 0], (down, high)),
                remote(cor_send.at[p, 1], cor_recv.at[p, 1], (up, high)),
            ]
            step.low = [
                remote(cor_send.at[p, 2], cor_recv.at[p, 2], (down, low)),
                remote(cor_send.at[p, 3], cor_recv.at[p, 3], (up, low)),
            ]
        count = 2 * len(to_low)
        step.low.insert(0, remote(vx_send.at[p, 0, pl.ds(0, count)], vx_high.at[p, pl.ds(0, count)], (d, low)))
        count = 2 * len(to_high)
        step.high.insert(0, remote(vx_send.at[p, 1, pl.ds(0, count)], vx_low.at[p, pl.ds(0, count)], (d, high)))
        step.start()
        return step

    def own_y_differences(p):
        v = vs.at[p]

        def body(z, carry):
            later = []
            for t in range(2):
                tile = Tile(row_of(z, 8 * t))
                parts = y_differences([tile.load(v, k) for k in range(3)])
                for k in range(3):
                    for h in range(2):
                        tile.store(later, gy, k, h, parts[k][h])
            write(later)
            return carry

        lax.fori_loop(0, NZ_OWN, body, 0, unroll=2)

    def take_velocity(p, step):
        own_y_differences(p)
        v = vs.at[p]
        wide = p < 2 * steps - 1
        to_low, to_high = (WIDE_LOW, WIDE_HIGH) if wide else (THIN_LOW, THIN_HIGH)
        step.wait_send()
        step.wait_recv()

        def clear(field, z, depth):
            def body(i, carry):
                v[field, pl.ds(row_of(z, 0) + 8 * i, 8), :] = zero
                return carry

            lax.fori_loop(0, depth * LAYER // 8, body, 0)

        @pl.when(top)
        def _():
            if wide:
                clear(0, -1, 1)
                clear(1, -1, 1)
                clear(2, -2, 2)
            else:
                clear(2, -1, 1)

        @pl.when(bottom)
        def _():
            for field in range(2):
                clear(field, NZ_OWN, 2 if wide else 1)
            if wide:
                clear(2, NZ_OWN, 1)

        for k, (field, here, there) in enumerate(to_low):
            for h in range(2):
                put_face(v, field, there, h, vx_high[p, 2 * k + h])
        for k, (field, here, there) in enumerate(to_high):
            for h in range(2):
                put_face(v, field, there, h, vx_low[p, 2 * k + h])
        if wide:
            for c, (x, z, outside) in enumerate(
                ((-1, -1, top), (-1, NZ_OWN, bottom), (NX_OWN, -1, top), (NX_OWN, NZ_OWN, bottom))
            ):
                for field in corner_fields[c]:
                    for h in range(2):
                        value = cor_recv[p, c, pl.ds(2 * field + h, 1), :]
                        v[field, pl.ds(row_of(z, x, h), 1), :] = jnp.where(outside, 0.0, value)

    rounds = []
    reach = 2
    while reach < nd // 2:
        rounds.append(reach)
        reach *= 2

    def far_signal(i):
        if i < len(rounds):
            for way, other in enumerate((lax.rem(d + rounds[i], nd), lax.rem(d + nd - rounds[i], nd))):
                pl.semaphore_signal(far_sem.at[2 * i + way], inc=1, device_id=(other, l), device_id_type=MESH)

    def far_wait(i):
        if i < len(rounds):
            for way in range(2):
                pl.semaphore_wait(far_sem.at[2 * i + way], 1)

    def note_surface(gain, w_slot, start):
        @pl.when(top)
        def _():
            for t in range(2):
                for h in range(2):
                    place = pl.ds(row_of(0, 8 * t, h), 8)
                    if w_slot is None:
                        value = sp[2, place, :]
                    else:
                        value = sp[2, place, :] - vs[w_slot, 2, place, :]
                    spot = pl.ds(16 * h + 8 * t, 8)
                    q_map[spot, :] = gain * value if start else q_map[spot, :] + gain * value

    y_copies = [remote(psum_buf.at[0], ysum_buf.at[l_y], (d, peer)) for peer in y_peers]
    x_copies = [remote(psum_buf.at[1], xsum_buf.at[l_x], (d, peer)) for peer in x_peers]

    def add_up_pulses():
        @pl.when(top)
        def _():
            bins = lax.broadcasted_iota(jnp.int32, (pulses, 128), 0)
            total = jnp.zeros((pulses, 128), F32)
            for t in range(2):
                for h in range(2):
                    foot = fp_ref[pl.ds(8 * t, 8), pl.ds(128 * h, 128)]
                    value = q_map[pl.ds(16 * h + 8 * t, 8), :]
                    for i in range(8):
                        total = total + jnp.where(
                            jnp.broadcast_to(foot[i : i + 1], (pulses, 128)) == bins,
                            jnp.broadcast_to(value[i : i + 1], (pulses, 128)),
                            0.0,
                        )
            sums = lax.dot_general(
                jnp.ones((8, 128), F32), total, (((1,), (1,)), ((), ())),
                precision=lax.Precision.HIGHEST, preferred_element_type=F32,
            )
            psum_buf[0] = zero
            psum_buf[0, :, pl.ds(0, pulses)] = sums
            for copy in y_copies:
                copy.start()
            ysum_buf[l_y] = psum_buf[0]
            for copy in y_copies:
                copy.wait_recv()
            sums = ysum_buf[0]
            for k in range(1, wide_y):
                sums = sums + ysum_buf[k]
            psum_buf[1] = sums
            for copy in x_copies:
                copy.start()
            xsum_buf[l_x] = sums
            for copy in y_copies:
                copy.wait_send()

    chips = nd // 2
    far = sorted(range(1, chips), key=lambda k: -min(k, chips - k))
    far_ids = [next(ids) for _ in far]
    core_id = next(ids)

    def spread_copy(k, send_id):
        return pltpu.make_async_remote_copy(
            src_ref=total_buf, dst_ref=total_buf, send_sem=send_sem.at[send_id], recv_sem=recv_sem.at[far_ids[0]],
            device_id=(2 * k, l), device_id_type=MESH,
        )

    core_copy = pltpu.make_async_remote_copy(
        src_ref=total_buf, dst_ref=total_buf, send_sem=send_sem.at[core_id], recv_sem=recv_sem.at[core_id],
        device_id=(d + 1 - 2 * lax.rem(d, 2), l), device_id_type=MESH,
    )
    scale = math.sqrt(pulses / (NX_OWN * nl * 256))

    def spread_pulses():
        @pl.when(top)
        def _():
            for copy in x_copies:
                copy.wait_recv()
            sums = xsum_buf[0]
            for k in range(1, n_x):
                sums = sums + xsum_buf[k]
            total_buf[...] = sums * scale
            for k, send_id in zip(far, far_ids):
                spread_copy(k, send_id).start()
            core_copy.start()
            for copy in x_copies:
                copy.wait_send()

    def finish_pulses():
        even = lax.rem(d, 2) == 0

        @pl.when(jnp.logical_and(even, jnp.logical_not(top)))
        def _():
            spread_copy(1, far_ids[0]).wait_recv()
            core_copy.start()

        @pl.when(jnp.logical_not(even))
        def _():
            core_copy.wait_recv()

        pulse_ref[...] = total_buf[pl.ds(0, 1), pl.ds(0, pulses)]

        @pl.when(even)
        def _():
            core_copy.wait_send()

        @pl.when(top)
        def _():
            for k, send_id in zip(far, far_ids):
                spread_copy(k, send_id).wait_send()

    note_surface(gains[steps - 1], None, True)
    first_faces.wait_recv()
    put_stress(((4, 5), (2,), (3, 4), (0,)))
    forward_velocity(0)
    step = send_velocity(0)
    far_signal(0)
    rest.wait_recv()
    put_stress(((0, 1, 2, 3), (0, 1, 3, 4, 5), (0, 1, 2, 5), (1, 2, 3, 4, 5)))
    for k in range(3):
        put_layer(cf, k, -1, zc_low.at[k], None)
        put_layer(cf, k, NZ_OWN, zc_high.at[k], None)
        put_layer(cf, 3 + k, -1, zm_low.at[k], None)
        put_layer(cf, 3 + k, NZ_OWN, zm_high.at[k], None)
    for k in range(6):
        for h in range(2):
            put_face(cf, k, -1, h, fx_low[12 + 2 * k + h])
            put_face(cf, k, NX_OWN, h, fx_high[12 + 2 * k + h])
    for h in range(2):
        load_map[pl.ds(BASE + GROUP * h - 1, 1), :] = fx_low[24, pl.ds(h, 1), :]
        load_map[pl.ds(BASE + GROUP * h + NX_OWN, 1), :] = fx_high[24, pl.ds(h, 1), :]
    for n in range(steps - 1):
        take_velocity(n, step)
        far_wait(n)
        forward_stress(n)
        forward_velocity(n + 1)
        step = send_velocity(n + 1)
        far_signal(n + 1)
        if n == 0:
            ends.wait_recv()
            for k in range(6):
                put_layer(sp, k, -1, zs_low.at[6 + k], None)
                put_layer(sp, k, NZ_OWN, zs_high.at[6 + k], None)
                for h in range(2):
                    put_face(sp, k, -1, h, fx_low[25 + 2 * k + h])
                    put_face(sp, k, NX_OWN, h, fx_high[25 + 2 * k + h])

    take_velocity(steps - 1, step)
    far_wait(steps - 1)
    turn()
    pulse_sends = []
    for n in range(steps - 1, -1, -1):
        backward_velocity(n)
        slot = 2 * steps - 1 - n
        step = send_velocity(slot)
        if n == 0:
            spread_pulses()
        if n > 0:
            note_surface(gains[n - 1], slot, False)
        if n == 1:
            add_up_pulses()
        take_velocity(slot, step)
        if n > 0:
            backward_stress(n - 1)

    def last_stress(z, carry):
        plain = []
        for t in range(2):
            tile = Tile(row_of(z, 8 * t))
            back = gradient(tile, vs.at[2 * steps - 1], gy)
            for h in range(2):
                for k in range(6):
                    plain.append(((3 + k,) + own(z, t, h), sp[k, tile.at(h), :] - back[h][k]))
        for place, value in plain:
            out_ref[place] = value
        return carry

    lax.fori_loop(0, NZ_OWN, last_stress, 0, unroll=UNROLL_S)
    finish_pulses()
    for exchange in (first_faces, rest, ends):
        exchange.wait_send()


def per_device(mesh_shape, checkpoint, end_cotangent, buoyancy, moduli, yield_radius, mask, footprint, amplitude):
    steps = mask.shape[0]
    pulses = amplitude.shape[0]
    nd, nl = mesh_shape
    phases = 2 * steps
    vmem = pltpu.VMEM
    ext = (ROWS, 128)
    tile = (8, 128)
    in_hbm = pl.BlockSpec(memory_space=pltpu.HBM)
    in_vmem = pl.BlockSpec(memory_space=pltpu.VMEM)
    scratch = [vmem(a.shape, a.dtype) for a in (checkpoint, end_cotangent, buoyancy, moduli, yield_radius, mask)]
    scratch += [vmem(footprint.shape, footprint.dtype), pltpu.SMEM(amplitude.shape, F32)]
    plane = checkpoint.shape[2:]
    scratch += [
        vmem((6,) + ext, F32),
        vmem((6,) + ext, F32),
        vmem((6,) + ext, F32),
        vmem((phases, 3) + ext, F32),
        vmem((3,) + buoyancy.shape, F32),
        vmem((steps - 1, 8) + ext, F32),
        vmem((3 + steps,) + ext, F32),
        vmem((3,) + ext, F32),
        vmem((64, 128), F32),
        vmem((32, 128), F32),
        vmem((2, 37) + tile, F32),
        vmem((37,) + tile, F32),
        vmem((37,) + tile, F32),
        vmem((12,) + plane, F32),
        vmem((12,) + plane, F32),
        vmem((3,) + plane, F32),
        vmem((3,) + plane, F32),
        vmem((steps,) + plane, jnp.int32),
        vmem((steps,) + plane, jnp.int32),
        vmem((phases, 2, 10) + tile, F32),
        vmem((phases, 10) + tile, F32),
        vmem((phases, 10) + tile, F32),
        vmem((phases - 1, 4) + tile, F32),
        vmem((phases - 1, 4) + tile, F32),
        vmem((2,) + tile, F32),
        vmem((4,) + tile, F32),
        vmem((4,) + tile, F32),
        vmem(tile, F32),
        pltpu.SemaphoreType.DMA((9,)),
        pltpu.SemaphoreType.DMA((112,)),
        pltpu.SemaphoreType.DMA((112,)),
        pltpu.SemaphoreType.REGULAR((8,)),
    ]
    adjoint, sums = pl.pallas_call(
        functools.partial(kernel, nd, nl, steps, pulses, 4),
        out_shape=(
            pltpu.VMEM(checkpoint.shape, F32),
            pltpu.VMEM((1, pulses), F32),
        ),
        in_specs=[in_hbm] * 8,
        out_specs=(in_vmem, in_vmem),
        scratch_shapes=scratch,
        compiler_params=pltpu.CompilerParams(
            collective_id=0, has_side_effects=True, vmem_limit_bytes=60 * 2**20
        ),
    )(checkpoint, end_cotangent, buoyancy, moduli, yield_radius, mask, footprint, amplitude)
    return adjoint, sums.reshape(pulses)


def solution(mesh):
    placed = (
        P(None, "depth", "lat", None),
        P(None, "depth", "lat", None),
        P("depth", "lat", None),
        P(None, "depth", "lat", None),
        P("depth", "lat", None),
        P(None, "depth", "lat", None),
        P("lat", None),
        P(),
    )
    return jax.shard_map(
        functools.partial(per_device, (mesh.shape["depth"], mesh.shape["lat"])),
        mesh=mesh,
        in_specs=placed,
        out_specs=(P(None, "depth", "lat", None), P()),
        check_vma=False,
    )
```

```python
import functools
import math

import jax
import jax.numpy as jnp
from jax import lax
from jax.experimental import pallas as pl
from jax.experimental.pallas import tpu as pltpu
from jax.sharding import PartitionSpec as P

MESH = pl.DeviceIdType.MESH
F32 = jnp.float32

NZ_OWN = 8
NX_OWN = 16
GROUP = 24
LAYER = 2 * GROUP
BASE = 8
UNROLL_S = 2
UNROLL_V = 8
UNROLL_H = 2
ROWS = BASE + (NZ_OWN + 4) * LAYER


def row_of(z, x, half=0):
    return BASE + LAYER * (z + 2) + GROUP * half + x


class Tile:
    def __init__(self, row, stride=1):
        self.row = row
        self.stride = stride

    def at(self, half, shift=0):
        start = self.row + GROUP * half + shift
        return pl.ds(start, 8) if self.stride == 1 else pl.ds(start, 8, self.stride)

    def load(self, ref, field, dz=0, dx=0):
        return [ref[field, self.at(half, LAYER * dz + dx), :] for half in range(2)]

    def store(self, later, ref, field, half, value):
        later.append((ref, field, self.at(half), value))


def y_shifts():
    lane = lax.broadcasted_iota(jnp.int32, (8, 128), 1)
    first = lane == 0
    last = lane == 127

    def before(pair):
        low, high = pltpu.roll(pair[0], 1, 1), pltpu.roll(pair[1], 1, 1)
        return [jnp.where(first, 0.0, low), jnp.where(first, low, high)]

    def after(pair):
        low, high = pltpu.roll(pair[0], 127, 1), pltpu.roll(pair[1], 127, 1)
        return [jnp.where(last, high, low), jnp.where(last, 0.0, high)]

    return before, after


def divergence(tile, ref):
    before, after = y_shifts()
    c = [tile.load(ref, k) for k in range(6)]
    xx_next = tile.load(ref, 0, dx=1)
    xy_prev = tile.load(ref, 3, dx=-1)
    xz_prev = tile.load(ref, 4, dx=-1)
    xz_up = tile.load(ref, 4, dz=-1)
    yz_up = tile.load(ref, 5, dz=-1)
    zz_down = tile.load(ref, 2, dz=1)
    xy_y = before(c[3])
    yz_y = before(c[5])
    yy_y = after(c[1])
    out = []
    for h in range(2):
        out.append(
            (
                (xx_next[h] - c[0][h]) + (c[3][h] - xy_y[h]) + (c[4][h] - xz_up[h]),
                (c[3][h] - xy_prev[h]) + (yy_y[h] - c[1][h]) + (c[5][h] - yz_up[h]),
                (c[4][h] - xz_prev[h]) + (c[5][h] - yz_y[h]) + (zz_down[h] - c[2][h]),
            )
        )
    return out


def y_differences(w):
    before, after = y_shifts()
    wy_y, wx_y, wz_y = before(w[1]), after(w[0]), after(w[2])
    return (
        [w[1][h] - wy_y[h] for h in range(2)],
        [wx_y[h] - w[0][h] for h in range(2)],
        [wz_y[h] - w[2][h] for h in range(2)],
    )


def gradient(tile, ref, along_y=None):
    w = [tile.load(ref, k) for k in range(3)]
    gy = y_differences(w) if along_y is None else [tile.load(along_y, k) for k in range(3)]
    wx_prev = tile.load(ref, 0, dx=-1)
    wz_up = tile.load(ref, 2, dz=-1)
    wy_next = tile.load(ref, 1, dx=1)
    wz_next = tile.load(ref, 2, dx=1)
    wx_down = tile.load(ref, 0, dz=1)
    wy_down = tile.load(ref, 1, dz=1)
    out = []
    for h in range(2):
        out.append(
            (
                w[0][h] - wx_prev[h],
                gy[0][h],
                w[2][h] - wz_up[h],
                gy[1][h] + (wy_next[h] - w[1][h]),
                (wx_down[h] - w[0][h]) + (wz_next[h] - w[2][h]),
                (wy_down[h] - w[1][h]) + gy[2][h],
            )
        )
    return out


def trial(s, e, lame, shear, limit, plastic):
    volume = lame * (e[0] + e[1] + e[2])
    twice = 2.0 * shear
    normal = [s[a] + volume + twice * e[a] for a in range(3)]
    shears = [s[a] + shear * e[a] for a in range(3, 6)]
    mean = (normal[0] + normal[1] + normal[2]) * (1.0 / 3.0)
    devs = [normal[a] - mean for a in range(3)]
    qsq = (devs[0] * devs[0] + devs[1] * devs[1] + devs[2] * devs[2]) + 2.0 * (
        shears[0] * shears[0] + shears[1] * shears[1] + shears[2] * shears[2]
    )
    inverse = lax.rsqrt(limit * limit + qsq)
    scaled = plastic * limit * inverse
    factor = (1.0 - plastic) + scaled
    slope = scaled * (inverse * inverse)
    return mean, devs + shears, factor, slope


def pull_back(g, parts, factor, slope, lame, shear):
    along = (g[0] * parts[0] + g[1] * parts[1] + g[2] * parts[2]) + (
        g[3] * parts[3] + g[4] * parts[4] + g[5] * parts[5]
    )
    pull = slope * along
    pull_twice = pull + pull
    total = g[0] + g[1] + g[2]
    rest = (1.0 - factor) * (total * (1.0 / 3.0))
    twice = 2.0 * shear
    volume = lame * total
    stress = [factor * g[a] - pull * parts[a] + rest for a in range(3)]
    stress += [factor * g[a] - pull_twice * parts[a] for a in range(3, 6)]
    strain = [volume + twice * stress[a] for a in range(3)]
    strain += [shear * stress[a] for a in range(3, 6)]
    return stress, strain


TO_LOW = (0, 1, 2, 3, 4, 5)
TO_HIGH = (3, 4, 0, 1, 2, 5)
WIDE_LOW = ((0, 0, 16), (1, 0, 16), (2, 0, 16), (1, 1, 17), (2, 1, 17))
WIDE_HIGH = ((0, 15, -1), (1, 15, -1), (2, 15, -1), (0, 14, -2))
THIN_LOW = ((1, 0, 16), (2, 0, 16))
THIN_HIGH = ((0, 15, -1),)


def kernel(
    nd, nl, steps, pulses,
    cp_in, ec_in, bu_in, mo_in, yi_in, ma_in, fp_in, amp_in,
    out_ref, pulse_ref,
    cp, ec, bu, mo, yi, ma, fp_ref, amp_ref,
    st, sp, co, vs, vb, hist, cf, gy,
    load_map, q_map, fx_send, fx_low, fx_high, zs_low, zs_high, zc_low, zc_high, zm_low, zm_high,
    vx_send, vx_low, vx_high, cor_send, cor_recv,
    psum_buf, sums_buf, total_buf,
    in_sem, send_sem, recv_sem, far_sem, lat_sem,
):
    d = lax.axis_index("depth")
    l = lax.axis_index("lat")
    top = d == 0
    bottom = d == nd - 1
    has_low = l > 0
    has_high = l < nl - 1
    up = lax.rem(d + nd - 1, nd)
    down = lax.rem(d + 1, nd)
    low = jnp.maximum(l - 1, 0)
    high = jnp.minimum(l + 1, nl - 1)
    gains = [math.sin(math.pi * (n + 0.5) / steps) for n in range(steps)]

    def load_in(k, source, target):
        copy = pltpu.make_async_copy(source, target, in_sem.at[k])
        copy.start()
        return copy

    stress_in = load_in(0, cp_in.at[pl.ds(3, 6)], cp.at[pl.ds(3, 6)])

    barrier = pltpu.get_barrier_semaphore()

    def greet(dd, ll):
        pl.semaphore_signal(barrier, inc=1, device_id=(dd, ll), device_id_type=MESH)

    greet(up, l)
    greet(down, l)

    @pl.when(has_low)
    def _():
        greet(d, low)

    @pl.when(has_high)
    def _():
        greet(d, high)

    others = ((mo_in, mo), (yi_in, yi), (ma_in, ma), (fp_in, fp_ref), (amp_in, amp_ref), (bu_in, bu), (ec_in, ec))
    static_in = [load_in(1 + k, source, target) for k, (source, target) in enumerate(others[:5])]
    velocity_in = load_in(6, cp_in.at[pl.ds(0, 3)], cp.at[pl.ds(0, 3)])
    late_in = [load_in(7 + k, source, target) for k, (source, target) in enumerate(others[5:])]
    ids = iter(range(1000))

    def remote(source, target, where):
        k = next(ids)
        return pltpu.make_async_remote_copy(
            src_ref=source, dst_ref=target, send_sem=send_sem.at[k], recv_sem=recv_sem.at[k],
            device_id=where, device_id_type=MESH,
        )

    def own(z, t, h):
        return (z, pl.ds(8 * t, 8), pl.ds(128 * h, 128))

    def stage_stress(z, carry):
        for t in range(2):
            for h in range(2):
                for k in range(6):
                    st[k, pl.ds(row_of(z, 8 * t, h), 8), :] = cp[(3 + k,) + own(z, t, h)]
        return carry

    def face(ref, field, x, h):
        return ref[field, pl.ds(row_of(0, x, h), NZ_OWN, LAYER), :]

    stress_in.wait()
    lax.fori_loop(0, NZ_OWN, stage_stress, 0)
    for side, order, x, count in ((0, TO_LOW, 0, 1), (1, TO_HIGH, NX_OWN - 1, 2)):
        for k in range(count):
            for h in range(2):
                fx_send[side, 2 * k + h] = face(st, order[k], x, h)

    pl.semaphore_wait(barrier, 2 + has_low.astype(jnp.int32) + has_high.astype(jnp.int32))

    class Exchange:
        def __init__(self):
            self.depth, self.low, self.high = [], [], []

        def start(self, more=None):
            more_low = more.low if more else []
            more_high = more.high if more else []

            @pl.when(has_low)
            def _():
                for copy in self.low + more_low:
                    copy.start()

            @pl.when(has_high)
            def _():
                for copy in self.high + more_high:
                    copy.start()

            for copy in self.depth:
                copy.start()

        def wait_send(self):
            for copy in self.depth:
                copy.wait_send()

            @pl.when(has_low)
            def _():
                for copy in self.low:
                    copy.wait_send()

            @pl.when(has_high)
            def _():
                for copy in self.high:
                    copy.wait_send()

        def wait_recv(self):
            for copy in self.depth:
                copy.wait_recv()

            @pl.when(has_high)
            def _():
                for copy in self.low:
                    copy.wait_recv()

            @pl.when(has_low)
            def _():
                for copy in self.high:
                    copy.wait_recv()

    last = NZ_OWN - 1
    first_faces = Exchange()
    first_faces.depth = [
        remote(cp.at[pl.ds(7, 2), last], zs_low.at[pl.ds(4, 2)], (down, l)),
        remote(cp.at[pl.ds(5, 1), 0], zs_high.at[pl.ds(2, 1)], (up, l)),
    ]
    first_faces.low = [remote(fx_send.at[0, pl.ds(0, 2)], fx_high.at[pl.ds(0, 2)], (d, low))]
    first_faces.high = [remote(fx_send.at[1, pl.ds(0, 4)], fx_low.at[pl.ds(0, 4)], (d, high))]
    first_faces.start()
    def stage(z, carry):
        for t in range(2):
            for h in range(2):
                place = pl.ds(row_of(z, 8 * t, h), 8)
                cf[0, place, :] = mo[(0,) + own(z, t, h)]
                cf[1, place, :] = mo[(1,) + own(z, t, h)]
                cf[2, place, :] = yi[own(z, t, h)]
                for k in range(3):
                    cf[3 + k, place, :] = ma[(k,) + own(z, t, h)].astype(F32)
        return carry

    def stage_end(z, carry):
        for t in range(2):
            for h in range(2):
                place = pl.ds(row_of(z, 8 * t, h), 8)
                for k in range(6):
                    sp[k, place, :] = ec[(3 + k,) + own(z, t, h)]
        return carry

    for copy in static_in:
        copy.wait()
    lax.fori_loop(0, NZ_OWN, stage, 0)

    load_map[...] = jnp.zeros_like(load_map)

    @pl.when(top)
    def _():
        for t in range(2):
            for h in range(2):
                foot = fp_ref[pl.ds(8 * t, 8), pl.ds(128 * h, 128)]

                def add(p, total, foot=foot):
                    return jnp.where(foot == p, amp_ref[p], total)

                load_map[pl.ds(BASE + GROUP * h + 8 * t, 8), :] = lax.fori_loop(
                    0, pulses, add, jnp.zeros((8, 128), F32), unroll=8
                )

    zero = jnp.zeros((8, 128), F32)

    @pl.when(jnp.logical_not(has_low))
    def _():
        fx_low[...] = jnp.zeros_like(fx_low)
        vx_low[...] = jnp.zeros_like(vx_low)
        for p in range(2 * steps - 1):
            cor_recv[p, 0] = zero
            cor_recv[p, 1] = zero

    @pl.when(jnp.logical_not(has_high))
    def _():
        fx_high[...] = jnp.zeros_like(fx_high)
        vx_high[...] = jnp.zeros_like(vx_high)
        for p in range(2 * steps - 1):
            cor_recv[p, 2] = zero
            cor_recv[p, 3] = zero

    for side, order, x, count in ((0, TO_LOW, 0, 1), (1, TO_HIGH, NX_OWN - 1, 2)):
        for k in range(count, 6):
            for h in range(2):
                fx_send[side, 2 * k + h] = face(st, order[k], x, h)
        for k in range(6):
            for h in range(2):
                fx_send[side, 12 + 2 * k + h] = face(cf, k, x, h)
        for h in range(2):
            fx_send[side, 24, pl.ds(h, 1), :] = load_map[pl.ds(BASE + GROUP * h + x, 1), :]

    rest = Exchange()
    rest.depth = [
        remote(cp.at[pl.ds(3, 4), last], zs_low.at[pl.ds(0, 4)], (down, l)),
        remote(mo.at[:, last], zc_low.at[pl.ds(0, 2)], (down, l)),
        remote(yi.at[pl.ds(last, 1)], zc_low.at[pl.ds(2, 1)], (down, l)),
        remote(ma.at[:, last], zm_low, (down, l)),
        remote(cp.at[pl.ds(3, 2), 0], zs_high.at[pl.ds(0, 2)], (up, l)),
        remote(cp.at[pl.ds(6, 3), 0], zs_high.at[pl.ds(3, 3)], (up, l)),
        remote(mo.at[:, 0], zc_high.at[pl.ds(0, 2)], (up, l)),
        remote(yi.at[pl.ds(0, 1)], zc_high.at[pl.ds(2, 1)], (up, l)),
        remote(ma.at[:, 0], zm_high, (up, l)),
    ]
    rest.low = [remote(fx_send.at[0, pl.ds(2, 23)], fx_high.at[pl.ds(2, 23)], (d, low))]
    rest.high = [remote(fx_send.at[1, pl.ds(4, 21)], fx_low.at[pl.ds(4, 21)], (d, high))]
    rest.start()

    velocity_in.wait()
    for copy in late_in:
        copy.wait()
    lax.fori_loop(0, NZ_OWN, stage_end, 0)
    for side, x in ((0, 0), (1, NX_OWN - 1)):
        for k in range(6):
            for h in range(2):
                fx_send[side, 25 + 2 * k + h] = face(sp, k, x, h)
    ends = Exchange()
    ends.depth = [
        remote(ec.at[pl.ds(3, 6), last], zs_low.at[pl.ds(6, 6)], (down, l)),
        remote(ec.at[pl.ds(3, 6), 0], zs_high.at[pl.ds(6, 6)], (up, l)),
    ]
    ends.low = [remote(fx_send.at[0, pl.ds(25, 12)], fx_high.at[pl.ds(25, 12)], (d, low))]
    ends.high = [remote(fx_send.at[1, pl.ds(25, 12)], fx_low.at[pl.ds(25, 12)], (d, high))]
    ends.start()

    def put_face(ref, field, x, h, value):
        ref[field, pl.ds(row_of(0, x, h), NZ_OWN, LAYER), :] = value

    def put_layer(ref, field, z, source, outside):
        for t in range(2):
            for h in range(2):
                value = source[pl.ds(8 * t, 8), pl.ds(128 * h, 128)].astype(F32)
                if outside is not None:
                    value = jnp.where(outside, 0.0, value)
                ref[field, pl.ds(row_of(z, 8 * t, h), 8), :] = value

    def put_stress(fields):
        for field in fields[0]:
            put_layer(st, field, -1, zs_low.at[field], top)
        for field in fields[1]:
            put_layer(st, field, NZ_OWN, zs_high.at[field], bottom)
        for field in fields[2]:
            for h in range(2):
                put_face(st, field, -1, h, fx_low[2 * TO_HIGH.index(field) + h])
        for field in fields[3]:
            for h in range(2):
                put_face(st, field, NX_OWN, h, fx_high[2 * TO_LOW.index(field) + h])

    inside_z = [jnp.logical_not(top), jnp.logical_not(bottom)]

    def write(later):
        for ref, field, place, value in later:
            ref[field, place, :] = value

    def everywhere(unit, take_corners):
        def inner(z, carry):
            later = []
            for t in range(2):
                unit(later, Tile(row_of(z, 8 * t)), None, gy)
            write(later)
            return carry

        lax.fori_loop(0, NZ_OWN, inner, 0, unroll=UNROLL_S)

        take_corners()

        def outer(side, carry):
            z = -1 + (NZ_OWN + 1) * side
            inside = jnp.where(side == 0, inside_z[0].astype(jnp.int32), inside_z[1].astype(jnp.int32)) > 0
            later = []
            for t in range(2):
                unit(later, Tile(row_of(z, 8 * t)), inside, None)
            write(later)
            return carry

        lax.fori_loop(0, 2, outer, 0, unroll=UNROLL_H)
        later = []
        unit(later, Tile(row_of(0, -1), LAYER), has_low, None)
        unit(later, Tile(row_of(0, NX_OWN), LAYER), has_high, None)
        write(later)

    def keep(inside, value):
        return value if inside is None else jnp.where(inside, value, 0.0)

    def coefficients(tile, n):
        return [tile.load(cf, k) for k in (0, 1, 2, 3 + n)]

    def forward_stress(n, take_corners):
        v = vs.at[n]
        record = hist.at[n]

        def unit(later, tile, inside, along_y):
            e = gradient(tile, v, along_y)
            s = [tile.load(st, k) for k in range(6)]
            lame, shear, limit, plastic = coefficients(tile, n)
            for h in range(2):
                mean, parts, factor, slope = trial(
                    [s[k][h] for k in range(6)], e[h], lame[h], shear[h], limit[h], plastic[h]
                )
                for k in range(6):
                    value = factor * parts[k]
                    if k < 3:
                        value = mean + value
                    tile.store(later, st, k, h, keep(inside, value))
                    tile.store(later, record, k, h, parts[k])
                tile.store(later, record, 6, h, factor)
                tile.store(later, record, 7, h, slope)

        everywhere(unit, take_corners)

        @pl.when(top)
        def _():
            for h in range(2):
                for x, count in ((-1, 1), (0, 8), (8, 8), (16, 1)):
                    place = pl.ds(row_of(0, x, h), count)
                    st[2, place, :] += gains[n] * load_map[pl.ds(BASE + GROUP * h + x, count), :]

    def turn(take_corners):
        n = steps - 1
        v = vs.at[n]

        def unit(later, tile, inside, along_y):
            e = gradient(tile, v, along_y)
            s = [tile.load(st, k) for k in range(6)]
            g = [tile.load(sp, k) for k in range(6)]
            lame, shear, limit, plastic = coefficients(tile, n)
            for h in range(2):
                mean, parts, factor, slope = trial(
                    [s[k][h] for k in range(6)], e[h], lame[h], shear[h], limit[h], plastic[h]
                )
                stress, strain = pull_back([g[k][h] for k in range(6)], parts, factor, slope, lame[h], shear[h])
                for k in range(6):
                    tile.store(later, sp, k, h, stress[k])
                    tile.store(later, co, k, h, keep(inside, strain[k]))

        everywhere(unit, take_corners)

    def backward_stress(n, take_corners):
        w = vs.at[2 * steps - 2 - n]
        record = hist.at[n]

        def unit(later, tile, inside, along_y):
            back = gradient(tile, w, along_y)
            s = [tile.load(sp, k) for k in range(6)]
            kept = [tile.load(record, k) for k in range(8)]
            lame, shear = tile.load(cf, 0), tile.load(cf, 1)
            for h in range(2):
                g = [s[k][h] - back[h][k] for k in range(6)]
                stress, strain = pull_back(
                    g, [kept[k][h] for k in range(6)], kept[6][h], kept[7][h], lame[h], shear[h]
                )
                for k in range(6):
                    tile.store(later, sp, k, h, stress[k])
                    tile.store(later, co, k, h, keep(inside, strain[k]))

        everywhere(unit, take_corners)

    def forward_velocity(n):
        def body(z, carry):
            later = []
            for t in range(2):
                tile = Tile(row_of(z, 8 * t))
                div = divergence(tile, st)
                for h in range(2):
                    b = bu[own(z, t, h)]
                    for k in range(3):
                        old = cp[(k,) + own(z, t, h)] if n == 0 else vs[n - 1, k, tile.at(h), :]
                        tile.store(later, vs.at[n], k, h, old + b * div[h][k])
            write(later)
            return carry

        lax.fori_loop(0, NZ_OWN, body, 0, unroll=UNROLL_V)

    def backward_velocity(n):
        slot = 2 * steps - 1 - n

        def body(z, carry):
            later = []
            plain = []
            for t in range(2):
                tile = Tile(row_of(z, 8 * t))
                div = divergence(tile, co)
                for h in range(2):
                    b = bu[own(z, t, h)]
                    for k in range(3):
                        source = ec if n == steps - 1 else vb
                        new = source[(k,) + own(z, t, h)] - div[h][k]
                        plain.append(((k,) + own(z, t, h), new))
                        tile.store(later, vs.at[slot], k, h, b * new)
            for place, new in plain:
                target = vb if n > 0 else out_ref
                target[place] = new
            write(later)
            return carry

        lax.fori_loop(0, NZ_OWN, body, 0, unroll=UNROLL_V)

    corner_fields = ((0, 2), (0, 1), (1, 2), (0, 1, 2))

    def send_velocity(p):
        v = vs.at[p]
        wide = p < 2 * steps - 1
        to_low, to_high = (WIDE_LOW, WIDE_HIGH) if wide else (THIN_LOW, THIN_HIGH)
        step, corners = Exchange(), Exchange()

        def layers(field, count, z, depth):
            return v.at[pl.ds(field, count), pl.ds(row_of(z, 0), depth * LAYER), :]

        if wide:
            step.depth = [
                remote(layers(0, 2, last, 1), layers(0, 2, -1, 1), (down, l)),
                remote(layers(2, 1, last - 1, 2), layers(2, 1, -2, 2), (down, l)),
                remote(layers(0, 2, 0, 2), layers(0, 2, NZ_OWN, 2), (up, l)),
                remote(layers(2, 1, 0, 1), layers(2, 1, NZ_OWN, 1), (up, l)),
            ]
        else:
            step.depth = [
                remote(layers(2, 1, last, 1), layers(2, 1, -1, 1), (down, l)),
                remote(layers(0, 2, 0, 1), layers(0, 2, NZ_OWN, 1), (up, l)),
            ]
        for k, (field, here, there) in enumerate(to_low):
            for h in range(2):
                vx_send[p, 0, 2 * k + h] = face(v, field, here, h)
        for k, (field, here, there) in enumerate(to_high):
            for h in range(2):
                vx_send[p, 1, 2 * k + h] = face(v, field, here, h)
        if wide:
            for c, (x, z) in enumerate(((15, last), (15, 0), (0, last), (0, 0))):
                for field in corner_fields[c]:
                    for h in range(2):
                        cor_send[p, c, pl.ds(2 * field + h, 1), :] = v[field, pl.ds(row_of(z, x, h), 1), :]
            corners.high = [
                remote(cor_send.at[p, 0], cor_recv.at[p, 0], (down, high)),
                remote(cor_send.at[p, 1], cor_recv.at[p, 1], (up, high)),
            ]
            corners.low = [
                remote(cor_send.at[p, 2], cor_recv.at[p, 2], (down, low)),
                remote(cor_send.at[p, 3], cor_recv.at[p, 3], (up, low)),
            ]
        count = 2 * len(to_low)
        step.low.append(remote(vx_send.at[p, 0, pl.ds(0, count)], vx_high.at[p, pl.ds(0, count)], (d, low)))
        count = 2 * len(to_high)
        step.high.append(remote(vx_send.at[p, 1, pl.ds(0, count)], vx_low.at[p, pl.ds(0, count)], (d, high)))
        step.start(corners)
        return step, corners

    def own_y_differences(p):
        v = vs.at[p]

        def body(z, carry):
            later = []
            for t in range(2):
                tile = Tile(row_of(z, 8 * t))
                parts = y_differences([tile.load(v, k) for k in range(3)])
                for k in range(3):
                    for h in range(2):
                        tile.store(later, gy, k, h, parts[k][h])
            write(later)
            return carry

        lax.fori_loop(0, NZ_OWN, body, 0, unroll=2)

    def take_velocity(p, step):
        step, corners = step
        own_y_differences(p)
        v = vs.at[p]
        wide = p < 2 * steps - 1
        to_low, to_high = (WIDE_LOW, WIDE_HIGH) if wide else (THIN_LOW, THIN_HIGH)
        step.wait_send()
        if wide:
            corners.wait_send()
        step.wait_recv()

        def clear(field, z, depth):
            def body(i, carry):
                v[field, pl.ds(row_of(z, 0) + 8 * i, 8), :] = zero
                return carry

            lax.fori_loop(0, depth * LAYER // 8, body, 0)

        @pl.when(top)
        def _():
            if wide:
                clear(0, -1, 1)
                clear(1, -1, 1)
                clear(2, -2, 2)
            else:
                clear(2, -1, 1)

        @pl.when(bottom)
        def _():
            for field in range(2):
                clear(field, NZ_OWN, 2 if wide else 1)
            if wide:
                clear(2, NZ_OWN, 1)

        for k, (field, here, there) in enumerate(to_low):
            for h in range(2):
                put_face(v, field, there, h, vx_high[p, 2 * k + h])
        for k, (field, here, there) in enumerate(to_high):
            for h in range(2):
                put_face(v, field, there, h, vx_low[p, 2 * k + h])
        def take_corners():
            corners.wait_recv()
            for c, (x, z, outside) in enumerate(
                ((-1, -1, top), (-1, NZ_OWN, bottom), (NX_OWN, -1, top), (NX_OWN, NZ_OWN, bottom))
            ):
                for field in corner_fields[c]:
                    for h in range(2):
                        value = cor_recv[p, c, pl.ds(2 * field + h, 1), :]
                        v[field, pl.ds(row_of(z, x, h), 1), :] = jnp.where(outside, 0.0, value)

        return take_corners

    rounds = []
    reach = 2
    while reach < nd // 2:
        rounds.append(reach)
        reach *= 2

    def far_signal(i):
        if i < len(rounds):
            for way, other in enumerate((lax.rem(d + rounds[i], nd), lax.rem(d + nd - rounds[i], nd))):
                pl.semaphore_signal(far_sem.at[2 * i + way], inc=1, device_id=(other, l), device_id_type=MESH)

            @pl.when(jnp.logical_and(top, l + rounds[i] < nl))
            def _():
                pl.semaphore_signal(lat_sem.at[2 * i], inc=1, device_id=(d, l + rounds[i]), device_id_type=MESH)

            @pl.when(jnp.logical_and(top, l >= rounds[i]))
            def _():
                pl.semaphore_signal(lat_sem.at[2 * i + 1], inc=1, device_id=(d, l - rounds[i]), device_id_type=MESH)

    def far_wait(i):
        if i < len(rounds):
            for way in range(2):
                pl.semaphore_wait(far_sem.at[2 * i + way], 1)

            @pl.when(jnp.logical_and(top, l >= rounds[i]))
            def _():
                pl.semaphore_wait(lat_sem.at[2 * i], 1)

            @pl.when(jnp.logical_and(top, l + rounds[i] < nl))
            def _():
                pl.semaphore_wait(lat_sem.at[2 * i + 1], 1)

    def note_surface(gain, w_slot, start):
        @pl.when(top)
        def _():
            for t in range(2):
                for h in range(2):
                    place = pl.ds(row_of(0, 8 * t, h), 8)
                    if w_slot is None:
                        value = sp[2, place, :]
                    else:
                        value = sp[2, place, :] - vs[w_slot, 2, place, :]
                    spot = pl.ds(16 * h + 8 * t, 8)
                    q_map[spot, :] = gain * value if start else q_map[spot, :] + gain * value

    peer_copies = [remote(psum_buf, sums_buf.at[l], (d, lax.rem(l + k, nl))) for k in range(1, nl)]

    def add_up_pulses():
        @pl.when(top)
        def _():
            bins = lax.broadcasted_iota(jnp.int32, (pulses, 128), 0)
            total = jnp.zeros((pulses, 128), F32)
            for t in range(2):
                for h in range(2):
                    foot = fp_ref[pl.ds(8 * t, 8), pl.ds(128 * h, 128)]
                    value = q_map[pl.ds(16 * h + 8 * t, 8), :]
                    for i in range(8):
                        total = total + jnp.where(
                            jnp.broadcast_to(foot[i : i + 1], (pulses, 128)) == bins,
                            jnp.broadcast_to(value[i : i + 1], (pulses, 128)),
                            0.0,
                        )
            sums = lax.dot_general(
                jnp.ones((8, 128), F32), total, (((1,), (1,)), ((), ())),
                precision=lax.Precision.HIGHEST, preferred_element_type=F32,
            )
            psum_buf[...] = zero
            psum_buf[:, pl.ds(0, pulses)] = sums
            for copy in peer_copies:
                copy.start()
            sums_buf[l] = psum_buf[...]

    far = sorted(range(1, nd), key=lambda k: -min(k // 2, nd // 2 - k // 2))
    far_ids = [next(ids) for _ in far]

    def spread_copy(k, send_id):
        return pltpu.make_async_remote_copy(
            src_ref=total_buf, dst_ref=total_buf, send_sem=send_sem.at[send_id], recv_sem=recv_sem.at[far_ids[0]],
            device_id=(k, l), device_id_type=MESH,
        )

    scale = math.sqrt(pulses / (NX_OWN * nl * 256))

    def spread_pulses():
        @pl.when(top)
        def _():
            for copy in peer_copies:
                copy.wait_recv()
            sums = sums_buf[0]
            for k in range(1, nl):
                sums = sums + sums_buf[k]
            total_buf[...] = sums * scale
            for k, send_id in zip(far, far_ids):
                spread_copy(k, send_id).start()

    def finish_pulses():
        @pl.when(jnp.logical_not(top))
        def _():
            spread_copy(1, far_ids[0]).wait_recv()

        pulse_ref[...] = total_buf[pl.ds(0, 1), pl.ds(0, pulses)]

        @pl.when(top)
        def _():
            for copy in peer_copies:
                copy.wait_send()
            for k, send_id in zip(far, far_ids):
                spread_copy(k, send_id).wait_send()

    note_surface(gains[steps - 1], None, True)
    first_faces.wait_recv()
    put_stress(((4, 5), (2,), (3, 4), (0,)))
    forward_velocity(0)
    step = send_velocity(0)
    far_signal(0)
    rest.wait_recv()
    put_stress(((0, 1, 2, 3), (0, 1, 3, 4, 5), (0, 1, 2, 5), (1, 2, 3, 4, 5)))
    for k in range(3):
        put_layer(cf, k, -1, zc_low.at[k], None)
        put_layer(cf, k, NZ_OWN, zc_high.at[k], None)
        put_layer(cf, 3 + k, -1, zm_low.at[k], None)
        put_layer(cf, 3 + k, NZ_OWN, zm_high.at[k], None)
    for k in range(6):
        for h in range(2):
            put_face(cf, k, -1, h, fx_low[12 + 2 * k + h])
            put_face(cf, k, NX_OWN, h, fx_high[12 + 2 * k + h])
    for h in range(2):
        load_map[pl.ds(BASE + GROUP * h - 1, 1), :] = fx_low[24, pl.ds(h, 1), :]
        load_map[pl.ds(BASE + GROUP * h + NX_OWN, 1), :] = fx_high[24, pl.ds(h, 1), :]
    for n in range(steps - 1):
        take_corners = take_velocity(n, step)
        far_wait(n)
        forward_stress(n, take_corners)
        forward_velocity(n + 1)
        step = send_velocity(n + 1)
        far_signal(n + 1)
        if n == 0:
            ends.wait_recv()
            for k in range(6):
                put_layer(sp, k, -1, zs_low.at[6 + k], None)
                put_layer(sp, k, NZ_OWN, zs_high.at[6 + k], None)
                for h in range(2):
                    put_face(sp, k, -1, h, fx_low[25 + 2 * k + h])
                    put_face(sp, k, NX_OWN, h, fx_high[25 + 2 * k + h])

    take_corners = take_velocity(steps - 1, step)
    far_wait(steps - 1)
    turn(take_corners)
    pulse_sends = []
    for n in range(steps - 1, -1, -1):
        backward_velocity(n)
        slot = 2 * steps - 1 - n
        step = send_velocity(slot)
        if n == 0:
            spread_pulses()
        if n > 0:
            note_surface(gains[n - 1], slot, False)
        if n == 1:
            add_up_pulses()
        take_corners = take_velocity(slot, step)
        if n > 0:
            backward_stress(n - 1, take_corners)

    def last_stress(z, carry):
        plain = []
        for t in range(2):
            tile = Tile(row_of(z, 8 * t))
            back = gradient(tile, vs.at[2 * steps - 1], gy)
            for h in range(2):
                for k in range(6):
                    plain.append(((3 + k,) + own(z, t, h), sp[k, tile.at(h), :] - back[h][k]))
        for place, value in plain:
            out_ref[place] = value
        return carry

    lax.fori_loop(0, NZ_OWN, last_stress, 0, unroll=UNROLL_S)
    finish_pulses()
    for exchange in (first_faces, rest, ends):
        exchange.wait_send()


def per_device(mesh_shape, checkpoint, end_cotangent, buoyancy, moduli, yield_radius, mask, footprint, amplitude):
    steps = mask.shape[0]
    pulses = amplitude.shape[0]
    nd, nl = mesh_shape
    phases = 2 * steps
    vmem = pltpu.VMEM
    ext = (ROWS, 128)
    tile = (8, 128)
    in_hbm = pl.BlockSpec(memory_space=pltpu.HBM)
    in_vmem = pl.BlockSpec(memory_space=pltpu.VMEM)
    scratch = [vmem(a.shape, a.dtype) for a in (checkpoint, end_cotangent, buoyancy, moduli, yield_radius, mask)]
    scratch += [vmem(footprint.shape, footprint.dtype), pltpu.SMEM(amplitude.shape, F32)]
    plane = checkpoint.shape[2:]
    scratch += [
        vmem((6,) + ext, F32),
        vmem((6,) + ext, F32),
        vmem((6,) + ext, F32),
        vmem((phases, 3) + ext, F32),
        vmem((3,) + buoyancy.shape, F32),
        vmem((steps - 1, 8) + ext, F32),
        vmem((3 + steps,) + ext, F32),
        vmem((3,) + ext, F32),
        vmem((64, 128), F32),
        vmem((32, 128), F32),
        vmem((2, 37) + tile, F32),
        vmem((37,) + tile, F32),
        vmem((37,) + tile, F32),
        vmem((12,) + plane, F32),
        vmem((12,) + plane, F32),
        vmem((3,) + plane, F32),
        vmem((3,) + plane, F32),
        vmem((steps,) + plane, jnp.int32),
        vmem((steps,) + plane, jnp.int32),
        vmem((phases, 2, 10) + tile, F32),
        vmem((phases, 10) + tile, F32),
        vmem((phases, 10) + tile, F32),
        vmem((phases - 1, 4) + tile, F32),
        vmem((phases - 1, 4) + tile, F32),
        vmem(tile, F32),
        vmem((nl,) + tile, F32),
        vmem(tile, F32),
        pltpu.SemaphoreType.DMA((9,)),
        pltpu.SemaphoreType.DMA((128,)),
        pltpu.SemaphoreType.DMA((128,)),
        pltpu.SemaphoreType.REGULAR((8,)),
        pltpu.SemaphoreType.REGULAR((8,)),
    ]
    adjoint, sums = pl.pallas_call(
        functools.partial(kernel, nd, nl, steps, pulses),
        out_shape=(
            pltpu.VMEM(checkpoint.shape, F32),
            pltpu.VMEM((1, pulses), F32),
        ),
        in_specs=[in_hbm] * 8,
        out_specs=(in_vmem, in_vmem),
        scratch_shapes=scratch,
        compiler_params=pltpu.CompilerParams(
            collective_id=0, has_side_effects=True, vmem_limit_bytes=60 * 2**20
        ),
    )(checkpoint, end_cotangent, buoyancy, moduli, yield_radius, mask, footprint, amplitude)
    return adjoint, sums.reshape(pulses)


def solution(mesh):
    placed = (
        P(None, "depth", "lat", None),
        P(None, "depth", "lat", None),
        P("depth", "lat", None),
        P(None, "depth", "lat", None),
        P("depth", "lat", None),
        P(None, "depth", "lat", None),
        P("lat", None),
        P(),
    )
    return jax.shard_map(
        functools.partial(per_device, (mesh.shape["depth"], mesh.shape["lat"])),
        mesh=mesh,
        in_specs=placed,
        out_specs=(P(None, "depth", "lat", None), P()),
        check_vma=False,
    )
```

```python
import functools
import math

import jax
import jax.numpy as jnp
from jax import lax
from jax.experimental import pallas as pl
from jax.experimental.pallas import tpu as pltpu
from jax.sharding import PartitionSpec as P

MESH = pl.DeviceIdType.MESH
F32 = jnp.float32

NZ_OWN = 8
NX_OWN = 16
GROUP = 24
LAYER = 2 * GROUP
BASE = 8
UNROLL_S = 2
UNROLL_V = 8
UNROLL_H = 2
ROWS = BASE + (NZ_OWN + 4) * LAYER


def row_of(z, x, half=0):
    return BASE + LAYER * (z + 2) + GROUP * half + x


class Tile:
    def __init__(self, row, stride=1):
        self.row = row
        self.stride = stride

    def at(self, half, shift=0):
        start = self.row + GROUP * half + shift
        return pl.ds(start, 8) if self.stride == 1 else pl.ds(start, 8, self.stride)

    def load(self, ref, field, dz=0, dx=0):
        return [ref[field, self.at(half, LAYER * dz + dx), :] for half in range(2)]

    def store(self, later, ref, field, half, value):
        later.append((ref, field, self.at(half), value))


def y_shifts():
    lane = lax.broadcasted_iota(jnp.int32, (8, 128), 1)
    first = lane == 0
    last = lane == 127

    def before(pair):
        low, high = pltpu.roll(pair[0], 1, 1), pltpu.roll(pair[1], 1, 1)
        return [jnp.where(first, 0.0, low), jnp.where(first, low, high)]

    def after(pair):
        low, high = pltpu.roll(pair[0], 127, 1), pltpu.roll(pair[1], 127, 1)
        return [jnp.where(last, high, low), jnp.where(last, 0.0, high)]

    return before, after


def divergence(tile, ref):
    before, after = y_shifts()
    c = [tile.load(ref, k) for k in range(6)]
    xx_next = tile.load(ref, 0, dx=1)
    xy_prev = tile.load(ref, 3, dx=-1)
    xz_prev = tile.load(ref, 4, dx=-1)
    xz_up = tile.load(ref, 4, dz=-1)
    yz_up = tile.load(ref, 5, dz=-1)
    zz_down = tile.load(ref, 2, dz=1)
    xy_y = before(c[3])
    yz_y = before(c[5])
    yy_y = after(c[1])
    out = []
    for h in range(2):
        out.append(
            (
                (xx_next[h] - c[0][h]) + (c[3][h] - xy_y[h]) + (c[4][h] - xz_up[h]),
                (c[3][h] - xy_prev[h]) + (yy_y[h] - c[1][h]) + (c[5][h] - yz_up[h]),
                (c[4][h] - xz_prev[h]) + (c[5][h] - yz_y[h]) + (zz_down[h] - c[2][h]),
            )
        )
    return out


def y_differences(w):
    before, after = y_shifts()
    wy_y, wx_y, wz_y = before(w[1]), after(w[0]), after(w[2])
    return (
        [w[1][h] - wy_y[h] for h in range(2)],
        [wx_y[h] - w[0][h] for h in range(2)],
        [wz_y[h] - w[2][h] for h in range(2)],
    )


def gradient(tile, ref, along_y=None):
    w = [tile.load(ref, k) for k in range(3)]
    gy = y_differences(w) if along_y is None else [tile.load(along_y, k) for k in range(3)]
    wx_prev = tile.load(ref, 0, dx=-1)
    wz_up = tile.load(ref, 2, dz=-1)
    wy_next = tile.load(ref, 1, dx=1)
    wz_next = tile.load(ref, 2, dx=1)
    wx_down = tile.load(ref, 0, dz=1)
    wy_down = tile.load(ref, 1, dz=1)
    out = []
    for h in range(2):
        out.append(
            (
                w[0][h] - wx_prev[h],
                gy[0][h],
                w[2][h] - wz_up[h],
                gy[1][h] + (wy_next[h] - w[1][h]),
                (wx_down[h] - w[0][h]) + (wz_next[h] - w[2][h]),
                (wy_down[h] - w[1][h]) + gy[2][h],
            )
        )
    return out


def trial(s, e, lame, shear, limit, plastic):
    volume = lame * (e[0] + e[1] + e[2])
    twice = 2.0 * shear
    normal = [s[a] + volume + twice * e[a] for a in range(3)]
    shears = [s[a] + shear * e[a] for a in range(3, 6)]
    mean = (normal[0] + normal[1] + normal[2]) * (1.0 / 3.0)
    devs = [normal[a] - mean for a in range(3)]
    qsq = (devs[0] * devs[0] + devs[1] * devs[1] + devs[2] * devs[2]) + 2.0 * (
        shears[0] * shears[0] + shears[1] * shears[1] + shears[2] * shears[2]
    )
    inverse = lax.rsqrt(limit * limit + qsq)
    scaled = plastic * limit * inverse
    factor = (1.0 - plastic) + scaled
    slope = scaled * (inverse * inverse)
    return mean, devs + shears, factor, slope


def pull_back(g, parts, factor, slope, lame, shear):
    along = (g[0] * parts[0] + g[1] * parts[1] + g[2] * parts[2]) + (
        g[3] * parts[3] + g[4] * parts[4] + g[5] * parts[5]
    )
    pull = slope * along
    pull_twice = pull + pull
    total = g[0] + g[1] + g[2]
    rest = (1.0 - factor) * (total * (1.0 / 3.0))
    twice = 2.0 * shear
    volume = lame * total
    stress = [factor * g[a] - pull * parts[a] + rest for a in range(3)]
    stress += [factor * g[a] - pull_twice * parts[a] for a in range(3, 6)]
    strain = [volume + twice * stress[a] for a in range(3)]
    strain += [shear * stress[a] for a in range(3, 6)]
    return stress, strain


TO_LOW = (0, 1, 2, 3, 4, 5)
TO_HIGH = (3, 4, 0, 1, 2, 5)
WIDE_LOW = ((1, 0, 16), (2, 0, 16), (0, 0, 16), (1, 1, 17), (2, 1, 17))
WIDE_HIGH = ((0, 15, -1), (1, 15, -1), (2, 15, -1), (0, 14, -2))
THIN_LOW = ((1, 0, 16), (2, 0, 16))
THIN_HIGH = ((0, 15, -1),)


def kernel(
    nd, nl, steps, pulses,
    cp_in, ec_in, bu_in, mo_in, yi_in, ma_in, fp_in, amp_in,
    out_ref, pulse_ref,
    cp, ec, bu, mo, yi, ma, fp_ref, amp_ref,
    st, sp, co, vs, vb, hist, cf, gy,
    load_map, q_map, fx_send, fx_low, fx_high, zs_low, zs_high, zc_low, zc_high, zm_low, zm_high,
    vx_send, vx_low, vx_high, cor_send, cor_recv,
    psum_buf, sums_buf, total_buf,
    in_sem, send_sem, recv_sem, far_sem, lat_sem,
):
    d = lax.axis_index("depth")
    l = lax.axis_index("lat")
    top = d == 0
    bottom = d == nd - 1
    has_low = l > 0
    has_high = l < nl - 1
    up = lax.rem(d + nd - 1, nd)
    down = lax.rem(d + 1, nd)
    low = jnp.maximum(l - 1, 0)
    high = jnp.minimum(l + 1, nl - 1)
    gains = [math.sin(math.pi * (n + 0.5) / steps) for n in range(steps)]

    def load_in(k, source, target):
        copy = pltpu.make_async_copy(source, target, in_sem.at[k])
        copy.start()
        return copy

    def load_rows(k, field, count, x, rows):
        part = (pl.ds(field, count), slice(None), pl.ds(x, rows))
        return load_in(k, cp_in.at[part], cp.at[part])

    low_in = load_rows(0, 3, 1, 0, 8)
    high_in = load_rows(9, 6, 2, 8, 8)
    stress_in = [load_rows(10, 7, 2, 0, 8), load_rows(11, 8, 1, 8, 8), load_rows(12, 4, 2, 0, 16), load_rows(13, 3, 1, 8, 8), load_rows(14, 6, 1, 0, 8)]

    barrier = pltpu.get_barrier_semaphore()

    def greet(dd, ll):
        pl.semaphore_signal(barrier, inc=1, device_id=(dd, ll), device_id_type=MESH)

    greet(up, l)
    greet(down, l)

    @pl.when(has_low)
    def _():
        greet(d, low)

    @pl.when(has_high)
    def _():
        greet(d, high)

    others = ((mo_in, mo), (yi_in, yi), (ma_in, ma), (fp_in, fp_ref), (amp_in, amp_ref), (bu_in, bu), (ec_in, ec))
    static_in = [load_in(1 + k, source, target) for k, (source, target) in enumerate(others[:5])]
    velocity_in = load_in(6, cp_in.at[pl.ds(0, 3)], cp.at[pl.ds(0, 3)])
    late_in = [load_in(7 + k, source, target) for k, (source, target) in enumerate(others[5:])]
    ids = iter(range(1000))

    def remote(source, target, where):
        k = next(ids)
        return pltpu.make_async_remote_copy(
            src_ref=source, dst_ref=target, send_sem=send_sem.at[k], recv_sem=recv_sem.at[k],
            device_id=where, device_id_type=MESH,
        )

    def own(z, t, h):
        return (z, pl.ds(8 * t, 8), pl.ds(128 * h, 128))

    first_parts = ((0, 0), (3, 1), (4, 1))

    def stage_parts(parts):
        def body(z, carry):
            for k, t in parts:
                for h in range(2):
                    st[k, pl.ds(row_of(z, 8 * t, h), 8), :] = cp[(3 + k,) + own(z, t, h)]
            return carry

        lax.fori_loop(0, NZ_OWN, body, 0)

    def face(ref, field, x, h):
        return ref[field, pl.ds(row_of(0, x, h), NZ_OWN, LAYER), :]

    low_in.wait()
    high_in.wait()
    stage_parts(first_parts)
    for side, order, x, count in ((0, TO_LOW, 0, 1), (1, TO_HIGH, NX_OWN - 1, 2)):
        for k in range(count):
            for h in range(2):
                fx_send[side, 2 * k + h] = face(st, order[k], x, h)

    pl.semaphore_wait(barrier, 2 + has_low.astype(jnp.int32) + has_high.astype(jnp.int32))

    class Exchange:
        def __init__(self):
            self.depth, self.low, self.high = [], [], []

        def start(self, more=None):
            self.start_x(more)
            self.start_depth(more)

        def start_x(self, more=None):
            more_low = more.low if more else []
            more_high = more.high if more else []

            @pl.when(has_low)
            def _():
                for copy in self.low + more_low:
                    copy.start()

            @pl.when(has_high)
            def _():
                for copy in self.high + more_high:
                    copy.start()

        def start_depth(self, more=None):
            for copy in self.depth + (more.depth if more else []):
                copy.start()

        def wait_send(self):
            for copy in self.depth:
                copy.wait_send()

            @pl.when(has_low)
            def _():
                for copy in self.low:
                    copy.wait_send()

            @pl.when(has_high)
            def _():
                for copy in self.high:
                    copy.wait_send()

        def wait_recv(self):
            for copy in self.depth:
                copy.wait_recv()

            @pl.when(has_high)
            def _():
                for copy in self.low:
                    copy.wait_recv()

            @pl.when(has_low)
            def _():
                for copy in self.high:
                    copy.wait_recv()

    last = NZ_OWN - 1
    first_faces = Exchange()
    first_faces.depth = [
        remote(cp.at[pl.ds(7, 2), last], zs_low.at[pl.ds(4, 2)], (down, l)),
        remote(cp.at[pl.ds(5, 1), 0], zs_high.at[pl.ds(2, 1)], (up, l)),
    ]
    first_faces.low = [remote(fx_send.at[0, pl.ds(0, 2)], fx_high.at[pl.ds(0, 2)], (d, low))]
    first_faces.high = [remote(fx_send.at[1, pl.ds(0, 4)], fx_low.at[pl.ds(0, 4)], (d, high))]
    first_faces.start_x()
    for copy in stress_in:
        copy.wait()
    first_faces.start_depth()
    stage_parts([(k, t) for k in range(6) for t in range(2) if (k, t) not in first_parts])
    def stage(z, carry):
        for t in range(2):
            for h in range(2):
                place = pl.ds(row_of(z, 8 * t, h), 8)
                cf[0, place, :] = mo[(0,) + own(z, t, h)]
                cf[1, place, :] = mo[(1,) + own(z, t, h)]
                cf[2, place, :] = yi[own(z, t, h)]
                for k in range(3):
                    cf[3 + k, place, :] = ma[(k,) + own(z, t, h)].astype(F32)
        return carry

    def stage_end(z, carry):
        for t in range(2):
            for h in range(2):
                place = pl.ds(row_of(z, 8 * t, h), 8)
                for k in range(6):
                    sp[k, place, :] = ec[(3 + k,) + own(z, t, h)]
        return carry

    for copy in static_in:
        copy.wait()
    lax.fori_loop(0, NZ_OWN, stage, 0)

    load_map[...] = jnp.zeros_like(load_map)

    @pl.when(top)
    def _():
        for t in range(2):
            for h in range(2):
                foot = fp_ref[pl.ds(8 * t, 8), pl.ds(128 * h, 128)]

                def add(p, total, foot=foot):
                    return jnp.where(foot == p, amp_ref[p], total)

                load_map[pl.ds(BASE + GROUP * h + 8 * t, 8), :] = lax.fori_loop(
                    0, pulses, add, jnp.zeros((8, 128), F32), unroll=8
                )

    zero = jnp.zeros((8, 128), F32)

    @pl.when(jnp.logical_not(has_low))
    def _():
        fx_low[...] = jnp.zeros_like(fx_low)
        vx_low[...] = jnp.zeros_like(vx_low)
        for p in range(2 * steps - 1):
            cor_recv[p, 0] = zero
            cor_recv[p, 1] = zero

    @pl.when(jnp.logical_not(has_high))
    def _():
        fx_high[...] = jnp.zeros_like(fx_high)
        vx_high[...] = jnp.zeros_like(vx_high)
        for p in range(2 * steps - 1):
            cor_recv[p, 2] = zero
            cor_recv[p, 3] = zero

    for side, order, x, count in ((0, TO_LOW, 0, 1), (1, TO_HIGH, NX_OWN - 1, 2)):
        for k in range(count, 6):
            for h in range(2):
                fx_send[side, 2 * k + h] = face(st, order[k], x, h)
        for k in range(6):
            for h in range(2):
                fx_send[side, 12 + 2 * k + h] = face(cf, k, x, h)
        for h in range(2):
            fx_send[side, 24, pl.ds(h, 1), :] = load_map[pl.ds(BASE + GROUP * h + x, 1), :]

    rest = Exchange()
    rest.depth = [
        remote(cp.at[pl.ds(3, 4), last], zs_low.at[pl.ds(0, 4)], (down, l)),
        remote(mo.at[:, last], zc_low.at[pl.ds(0, 2)], (down, l)),
        remote(yi.at[pl.ds(last, 1)], zc_low.at[pl.ds(2, 1)], (down, l)),
        remote(ma.at[:, last], zm_low, (down, l)),
        remote(cp.at[pl.ds(3, 2), 0], zs_high.at[pl.ds(0, 2)], (up, l)),
        remote(cp.at[pl.ds(6, 3), 0], zs_high.at[pl.ds(3, 3)], (up, l)),
        remote(mo.at[:, 0], zc_high.at[pl.ds(0, 2)], (up, l)),
        remote(yi.at[pl.ds(0, 1)], zc_high.at[pl.ds(2, 1)], (up, l)),
        remote(ma.at[:, 0], zm_high, (up, l)),
    ]
    rest.low = [remote(fx_send.at[0, pl.ds(2, 23)], fx_high.at[pl.ds(2, 23)], (d, low))]
    rest.high = [remote(fx_send.at[1, pl.ds(4, 21)], fx_low.at[pl.ds(4, 21)], (d, high))]
    rest.start()

    velocity_in.wait()
    for copy in late_in:
        copy.wait()
    lax.fori_loop(0, NZ_OWN, stage_end, 0)
    for side, x in ((0, 0), (1, NX_OWN - 1)):
        for k in range(6):
            for h in range(2):
                fx_send[side, 25 + 2 * k + h] = face(sp, k, x, h)
    ends = Exchange()
    ends.depth = [
        remote(ec.at[pl.ds(3, 6), last], zs_low.at[pl.ds(6, 6)], (down, l)),
        remote(ec.at[pl.ds(3, 6), 0], zs_high.at[pl.ds(6, 6)], (up, l)),
    ]
    ends.low = [remote(fx_send.at[0, pl.ds(25, 12)], fx_high.at[pl.ds(25, 12)], (d, low))]
    ends.high = [remote(fx_send.at[1, pl.ds(25, 12)], fx_low.at[pl.ds(25, 12)], (d, high))]
    ends.start()

    def put_face(ref, field, x, h, value):
        ref[field, pl.ds(row_of(0, x, h), NZ_OWN, LAYER), :] = value

    def put_layer(ref, field, z, source, outside):
        for t in range(2):
            for h in range(2):
                value = source[pl.ds(8 * t, 8), pl.ds(128 * h, 128)].astype(F32)
                if outside is not None:
                    value = jnp.where(outside, 0.0, value)
                ref[field, pl.ds(row_of(z, 8 * t, h), 8), :] = value

    def put_stress(fields):
        for field in fields[0]:
            put_layer(st, field, -1, zs_low.at[field], top)
        for field in fields[1]:
            put_layer(st, field, NZ_OWN, zs_high.at[field], bottom)
        for field in fields[2]:
            for h in range(2):
                put_face(st, field, -1, h, fx_low[2 * TO_HIGH.index(field) + h])
        for field in fields[3]:
            for h in range(2):
                put_face(st, field, NX_OWN, h, fx_high[2 * TO_LOW.index(field) + h])

    inside_z = [jnp.logical_not(top), jnp.logical_not(bottom)]

    def write(later):
        for ref, field, place, value in later:
            ref[field, place, :] = value

    def everywhere(unit, take_corners):
        def inner(z, carry):
            later = []
            for t in range(2):
                unit(later, Tile(row_of(z, 8 * t)), None, gy)
            write(later)
            return carry

        lax.fori_loop(0, NZ_OWN, inner, 0, unroll=UNROLL_S)

        take_corners()

        def outer(side, carry):
            z = -1 + (NZ_OWN + 1) * side
            inside = jnp.where(side == 0, inside_z[0].astype(jnp.int32), inside_z[1].astype(jnp.int32)) > 0
            later = []
            for t in range(2):
                unit(later, Tile(row_of(z, 8 * t)), inside, None)
            write(later)
            return carry

        lax.fori_loop(0, 2, outer, 0, unroll=UNROLL_H)
        later = []
        unit(later, Tile(row_of(0, -1), LAYER), has_low, None)
        unit(later, Tile(row_of(0, NX_OWN), LAYER), has_high, None)
        write(later)

    def keep(inside, value):
        return value if inside is None else jnp.where(inside, value, 0.0)

    def coefficients(tile, n):
        return [tile.load(cf, k) for k in (0, 1, 2, 3 + n)]

    def forward_stress(n, take_corners):
        v = vs.at[n]
        record = hist.at[n]

        def unit(later, tile, inside, along_y):
            e = gradient(tile, v, along_y)
            s = [tile.load(st, k) for k in range(6)]
            lame, shear, limit, plastic = coefficients(tile, n)
            for h in range(2):
                mean, parts, factor, slope = trial(
                    [s[k][h] for k in range(6)], e[h], lame[h], shear[h], limit[h], plastic[h]
                )
                for k in range(6):
                    value = factor * parts[k]
                    if k < 3:
                        value = mean + value
                    tile.store(later, st, k, h, keep(inside, value))
                    tile.store(later, record, k, h, parts[k])
                tile.store(later, record, 6, h, factor)
                tile.store(later, record, 7, h, slope)

        everywhere(unit, take_corners)

        @pl.when(top)
        def _():
            for h in range(2):
                for x, count in ((-1, 1), (0, 8), (8, 8), (16, 1)):
                    place = pl.ds(row_of(0, x, h), count)
                    st[2, place, :] += gains[n] * load_map[pl.ds(BASE + GROUP * h + x, count), :]

    def turn(take_corners):
        n = steps - 1
        v = vs.at[n]

        def unit(later, tile, inside, along_y):
            e = gradient(tile, v, along_y)
            s = [tile.load(st, k) for k in range(6)]
            g = [tile.load(sp, k) for k in range(6)]
            lame, shear, limit, plastic = coefficients(tile, n)
            for h in range(2):
                mean, parts, factor, slope = trial(
                    [s[k][h] for k in range(6)], e[h], lame[h], shear[h], limit[h], plastic[h]
                )
                stress, strain = pull_back([g[k][h] for k in range(6)], parts, factor, slope, lame[h], shear[h])
                for k in range(6):
                    tile.store(later, sp, k, h, stress[k])
                    tile.store(later, co, k, h, keep(inside, strain[k]))

        everywhere(unit, take_corners)

    def backward_stress(n, take_corners):
        w = vs.at[2 * steps - 2 - n]
        record = hist.at[n]

        def unit(later, tile, inside, along_y):
            back = gradient(tile, w, along_y)
            s = [tile.load(sp, k) for k in range(6)]
            kept = [tile.load(record, k) for k in range(8)]
            lame, shear = tile.load(cf, 0), tile.load(cf, 1)
            for h in range(2):
                g = [s[k][h] - back[h][k] for k in range(6)]
                stress, strain = pull_back(
                    g, [kept[k][h] for k in range(6)], kept[6][h], kept[7][h], lame[h], shear[h]
                )
                for k in range(6):
                    tile.store(later, sp, k, h, stress[k])
                    tile.store(later, co, k, h, keep(inside, strain[k]))

        everywhere(unit, take_corners)

    def forward_velocity(n):
        def body(z, carry):
            later = []
            for t in range(2):
                tile = Tile(row_of(z, 8 * t))
                div = divergence(tile, st)
                for h in range(2):
                    b = bu[own(z, t, h)]
                    for k in range(3):
                        old = cp[(k,) + own(z, t, h)] if n == 0 else vs[n - 1, k, tile.at(h), :]
                        tile.store(later, vs.at[n], k, h, old + b * div[h][k])
            write(later)
            return carry

        lax.fori_loop(0, NZ_OWN, body, 0, unroll=UNROLL_V)

    def backward_velocity(n):
        slot = 2 * steps - 1 - n

        def body(z, carry):
            later = []
            plain = []
            for t in range(2):
                tile = Tile(row_of(z, 8 * t))
                div = divergence(tile, co)
                for h in range(2):
                    b = bu[own(z, t, h)]
                    for k in range(3):
                        source = ec if n == steps - 1 else vb
                        new = source[(k,) + own(z, t, h)] - div[h][k]
                        plain.append(((k,) + own(z, t, h), new))
                        tile.store(later, vs.at[slot], k, h, b * new)
            for place, new in plain:
                target = vb if n > 0 else out_ref
                target[place] = new
            write(later)
            return carry

        lax.fori_loop(0, NZ_OWN, body, 0, unroll=UNROLL_V)

    corner_fields = ((0, 2), (0, 1), (1, 2), (0, 1, 2))

    def send_velocity(p):
        v = vs.at[p]
        wide = p < 2 * steps - 1
        to_low, to_high = (WIDE_LOW, WIDE_HIGH) if wide else (THIN_LOW, THIN_HIGH)
        step, corners = Exchange(), Exchange()

        def layer(field, count, here, there, where):
            return [
                remote(
                    v.at[pl.ds(field, count), pl.ds(row_of(here, 0), GROUP + NX_OWN), :],
                    v.at[pl.ds(field, count), pl.ds(row_of(there, 0), GROUP + NX_OWN), :],
                    where,
                )
            ]

        step.depth = layer(2, 1, last, -1, (down, l)) + layer(0, 2, 0, NZ_OWN, (up, l))
        if wide:
            corners.depth = layer(0, 2, last, -1, (down, l)) + layer(0, 2, 1, NZ_OWN + 1, (up, l))
            corners.depth += layer(2, 1, last - 1, -2, (down, l)) + layer(2, 1, 0, NZ_OWN, (up, l))
        for k, (field, here, there) in enumerate(to_low):
            for h in range(2):
                vx_send[p, 0, 2 * k + h] = face(v, field, here, h)
        for k, (field, here, there) in enumerate(to_high):
            for h in range(2):
                vx_send[p, 1, 2 * k + h] = face(v, field, here, h)
        if wide:
            for c, (x, z) in enumerate(((15, last), (15, 0), (0, last), (0, 0))):
                for field in corner_fields[c]:
                    for h in range(2):
                        cor_send[p, c, pl.ds(2 * field + h, 1), :] = v[field, pl.ds(row_of(z, x, h), 1), :]
            corners.high = [
                remote(cor_send.at[p, 0], cor_recv.at[p, 0], (down, high)),
                remote(cor_send.at[p, 1], cor_recv.at[p, 1], (up, high)),
            ]
            corners.low = [
                remote(cor_send.at[p, 2], cor_recv.at[p, 2], (down, low)),
                remote(cor_send.at[p, 3], cor_recv.at[p, 3], (up, low)),
            ]
        count = 2 * len(THIN_LOW)
        step.low.append(remote(vx_send.at[p, 0, pl.ds(0, count)], vx_high.at[p, pl.ds(0, count)], (d, low)))
        if wide:
            span = pl.ds(count, 2 * len(to_low) - count)
            corners.low.append(remote(vx_send.at[p, 0, span], vx_high.at[p, span], (d, low)))
        count = 2 * len(THIN_HIGH)
        step.high.append(remote(vx_send.at[p, 1, pl.ds(0, count)], vx_low.at[p, pl.ds(0, count)], (d, high)))
        if wide:
            span = pl.ds(count, 2 * len(to_high) - count)
            corners.high.append(remote(vx_send.at[p, 1, span], vx_low.at[p, span], (d, high)))
        step.start(corners)
        return step, corners

    def own_y_differences(p):
        v = vs.at[p]

        def body(z, carry):
            later = []
            for t in range(2):
                tile = Tile(row_of(z, 8 * t))
                parts = y_differences([tile.load(v, k) for k in range(3)])
                for k in range(3):
                    for h in range(2):
                        tile.store(later, gy, k, h, parts[k][h])
            write(later)
            return carry

        lax.fori_loop(0, NZ_OWN, body, 0, unroll=2)

    def take_velocity(p, step):
        step, corners = step
        own_y_differences(p)
        v = vs.at[p]
        wide = p < 2 * steps - 1
        to_low, to_high = (WIDE_LOW, WIDE_HIGH) if wide else (THIN_LOW, THIN_HIGH)
        step.wait_send()
        if wide:
            corners.wait_send()
        step.wait_recv()

        def clear(*places):
            for field, z in places:
                for t in range(2):
                    for h in range(2):
                        v[field, pl.ds(row_of(z, 8 * t, h), 8), :] = zero

        @pl.when(top)
        def _():
            clear((2, -1))

        @pl.when(bottom)
        def _():
            clear((0, NZ_OWN), (1, NZ_OWN))

        def put_faces(low_span, high_span):
            for k in low_span:
                field, here, there = to_low[k]
                for h in range(2):
                    put_face(v, field, there, h, vx_high[p, 2 * k + h])
            for k in high_span:
                field, here, there = to_high[k]
                for h in range(2):
                    put_face(v, field, there, h, vx_low[p, 2 * k + h])

        put_faces(range(len(THIN_LOW)), range(len(THIN_HIGH)))
        def take_corners():
            corners.wait_recv()

            @pl.when(top)
            def _():
                clear((0, -1), (1, -1), (2, -2))

            @pl.when(bottom)
            def _():
                clear((0, NZ_OWN + 1), (1, NZ_OWN + 1), (2, NZ_OWN))

            put_faces(range(len(THIN_LOW), len(to_low)), range(len(THIN_HIGH), len(to_high)))
            for c, (x, z, outside) in enumerate(
                ((-1, -1, top), (-1, NZ_OWN, bottom), (NX_OWN, -1, top), (NX_OWN, NZ_OWN, bottom))
            ):
                for field in corner_fields[c]:
                    for h in range(2):
                        value = cor_recv[p, c, pl.ds(2 * field + h, 1), :]
                        v[field, pl.ds(row_of(z, x, h), 1), :] = jnp.where(outside, 0.0, value)

        return take_corners

    rounds = []
    reach = 2
    while reach < nd // 2:
        rounds.append(reach)
        reach *= 2

    def far_signal(i):
        if i < len(rounds):
            for way, other in enumerate((lax.rem(d + rounds[i], nd), lax.rem(d + nd - rounds[i], nd))):
                pl.semaphore_signal(far_sem.at[2 * i + way], inc=1, device_id=(other, l), device_id_type=MESH)

            @pl.when(jnp.logical_and(top, l + rounds[i] < nl))
            def _():
                pl.semaphore_signal(lat_sem.at[2 * i], inc=1, device_id=(d, l + rounds[i]), device_id_type=MESH)

            @pl.when(jnp.logical_and(top, l >= rounds[i]))
            def _():
                pl.semaphore_signal(lat_sem.at[2 * i + 1], inc=1, device_id=(d, l - rounds[i]), device_id_type=MESH)

    def far_wait(i):
        if i < len(rounds):
            for way in range(2):
                pl.semaphore_wait(far_sem.at[2 * i + way], 1)

            @pl.when(jnp.logical_and(top, l >= rounds[i]))
            def _():
                pl.semaphore_wait(lat_sem.at[2 * i], 1)

            @pl.when(jnp.logical_and(top, l + rounds[i] < nl))
            def _():
                pl.semaphore_wait(lat_sem.at[2 * i + 1], 1)

    def note_surface(gain, w_slot, start):
        @pl.when(top)
        def _():
            for t in range(2):
                for h in range(2):
                    place = pl.ds(row_of(0, 8 * t, h), 8)
                    if w_slot is None:
                        value = sp[2, place, :]
                    else:
                        value = sp[2, place, :] - vs[w_slot, 2, place, :]
                    spot = pl.ds(16 * h + 8 * t, 8)
                    q_map[spot, :] = gain * value if start else q_map[spot, :] + gain * value

    peer_copies = [remote(psum_buf, sums_buf.at[l], (d, lax.rem(l + k, nl))) for k in range(1, nl)]

    def add_up_pulses():
        @pl.when(top)
        def _():
            bins = lax.broadcasted_iota(jnp.int32, (pulses, 128), 0)
            total = jnp.zeros((pulses, 128), F32)
            for t in range(2):
                for h in range(2):
                    foot = fp_ref[pl.ds(8 * t, 8), pl.ds(128 * h, 128)]
                    value = q_map[pl.ds(16 * h + 8 * t, 8), :]
                    for i in range(8):
                        total = total + jnp.where(
                            jnp.broadcast_to(foot[i : i + 1], (pulses, 128)) == bins,
                            jnp.broadcast_to(value[i : i + 1], (pulses, 128)),
                            0.0,
                        )
            sums = lax.dot_general(
                jnp.ones((8, 128), F32), total, (((1,), (1,)), ((), ())),
                precision=lax.Precision.HIGHEST, preferred_element_type=F32,
            )
            psum_buf[...] = zero
            psum_buf[:, pl.ds(0, pulses)] = sums
            for copy in peer_copies:
                copy.start()
            sums_buf[l] = psum_buf[...]

    far = sorted(range(1, nd), key=lambda k: -min(k // 2, nd // 2 - k // 2))
    far_ids = [next(ids) for _ in far]

    def spread_copy(k, send_id):
        return pltpu.make_async_remote_copy(
            src_ref=total_buf, dst_ref=total_buf, send_sem=send_sem.at[send_id], recv_sem=recv_sem.at[far_ids[0]],
            device_id=(k, l), device_id_type=MESH,
        )

    scale = math.sqrt(pulses / (NX_OWN * nl * 256))

    def spread_pulses():
        @pl.when(top)
        def _():
            for copy in peer_copies:
                copy.wait_recv()
            sums = sums_buf[0]
            for k in range(1, nl):
                sums = sums + sums_buf[k]
            total_buf[...] = sums * scale
            for k, send_id in zip(far, far_ids):
                spread_copy(k, send_id).start()

    def finish_pulses():
        @pl.when(jnp.logical_not(top))
        def _():
            spread_copy(1, far_ids[0]).wait_recv()

        pulse_ref[...] = total_buf[pl.ds(0, 1), pl.ds(0, pulses)]

        @pl.when(top)
        def _():
            for copy in peer_copies:
                copy.wait_send()
            for k, send_id in zip(far, far_ids):
                spread_copy(k, send_id).wait_send()

    note_surface(gains[steps - 1], None, True)
    first_faces.wait_recv()
    put_stress(((4, 5), (2,), (3, 4), (0,)))
    forward_velocity(0)
    step = send_velocity(0)
    far_signal(0)
    rest.wait_recv()
    put_stress(((0, 1, 2, 3), (0, 1, 3, 4, 5), (0, 1, 2, 5), (1, 2, 3, 4, 5)))
    for k in range(3):
        put_layer(cf, k, -1, zc_low.at[k], None)
        put_layer(cf, k, NZ_OWN, zc_high.at[k], None)
        put_layer(cf, 3 + k, -1, zm_low.at[k], None)
        put_layer(cf, 3 + k, NZ_OWN, zm_high.at[k], None)
    for k in range(6):
        for h in range(2):
            put_face(cf, k, -1, h, fx_low[12 + 2 * k + h])
            put_face(cf, k, NX_OWN, h, fx_high[12 + 2 * k + h])
    for h in range(2):
        load_map[pl.ds(BASE + GROUP * h - 1, 1), :] = fx_low[24, pl.ds(h, 1), :]
        load_map[pl.ds(BASE + GROUP * h + NX_OWN, 1), :] = fx_high[24, pl.ds(h, 1), :]
    for n in range(steps - 1):
        take_corners = take_velocity(n, step)
        far_wait(n)
        forward_stress(n, take_corners)
        forward_velocity(n + 1)
        step = send_velocity(n + 1)
        far_signal(n + 1)
        if n == 0:
            ends.wait_recv()
            for k in range(6):
                put_layer(sp, k, -1, zs_low.at[6 + k], None)
                put_layer(sp, k, NZ_OWN, zs_high.at[6 + k], None)
                for h in range(2):
                    put_face(sp, k, -1, h, fx_low[25 + 2 * k + h])
                    put_face(sp, k, NX_OWN, h, fx_high[25 + 2 * k + h])

    take_corners = take_velocity(steps - 1, step)
    far_wait(steps - 1)
    turn(take_corners)
    pulse_sends = []
    for n in range(steps - 1, -1, -1):
        backward_velocity(n)
        slot = 2 * steps - 1 - n
        step = send_velocity(slot)
        if n == 0:
            spread_pulses()
        if n > 0:
            note_surface(gains[n - 1], slot, False)
        if n == 1:
            add_up_pulses()
        take_corners = take_velocity(slot, step)
        if n > 0:
            backward_stress(n - 1, take_corners)

    def last_stress(z, carry):
        plain = []
        for t in range(2):
            tile = Tile(row_of(z, 8 * t))
            back = gradient(tile, vs.at[2 * steps - 1], gy)
            for h in range(2):
                for k in range(6):
                    plain.append(((3 + k,) + own(z, t, h), sp[k, tile.at(h), :] - back[h][k]))
        for place, value in plain:
            out_ref[place] = value
        return carry

    lax.fori_loop(0, NZ_OWN, last_stress, 0, unroll=UNROLL_S)
    finish_pulses()
    for exchange in (first_faces, rest, ends):
        exchange.wait_send()


def per_device(mesh_shape, checkpoint, end_cotangent, buoyancy, moduli, yield_radius, mask, footprint, amplitude):
    steps = mask.shape[0]
    pulses = amplitude.shape[0]
    nd, nl = mesh_shape
    phases = 2 * steps
    vmem = pltpu.VMEM
    ext = (ROWS, 128)
    tile = (8, 128)
    in_hbm = pl.BlockSpec(memory_space=pltpu.HBM)
    in_vmem = pl.BlockSpec(memory_space=pltpu.VMEM)
    scratch = [vmem(a.shape, a.dtype) for a in (checkpoint, end_cotangent, buoyancy, moduli, yield_radius, mask)]
    scratch += [vmem(footprint.shape, footprint.dtype), pltpu.SMEM(amplitude.shape, F32)]
    plane = checkpoint.shape[2:]
    scratch += [
        vmem((6,) + ext, F32),
        vmem((6,) + ext, F32),
        vmem((6,) + ext, F32),
        vmem((phases, 3) + ext, F32),
        vmem((3,) + buoyancy.shape, F32),
        vmem((steps - 1, 8) + ext, F32),
        vmem((3 + steps,) + ext, F32),
        vmem((3,) + ext, F32),
        vmem((64, 128), F32),
        vmem((32, 128), F32),
        vmem((2, 37) + tile, F32),
        vmem((37,) + tile, F32),
        vmem((37,) + tile, F32),
        vmem((12,) + plane, F32),
        vmem((12,) + plane, F32),
        vmem((3,) + plane, F32),
        vmem((3,) + plane, F32),
        vmem((steps,) + plane, jnp.int32),
        vmem((steps,) + plane, jnp.int32),
        vmem((phases, 2, 10) + tile, F32),
        vmem((phases, 10) + tile, F32),
        vmem((phases, 10) + tile, F32),
        vmem((phases - 1, 4) + tile, F32),
        vmem((phases - 1, 4) + tile, F32),
        vmem(tile, F32),
        vmem((nl,) + tile, F32),
        vmem(tile, F32),
        pltpu.SemaphoreType.DMA((15,)),
        pltpu.SemaphoreType.DMA((176,)),
        pltpu.SemaphoreType.DMA((176,)),
        pltpu.SemaphoreType.REGULAR((8,)),
        pltpu.SemaphoreType.REGULAR((8,)),
    ]
    adjoint, sums = pl.pallas_call(
        functools.partial(kernel, nd, nl, steps, pulses),
        out_shape=(
            pltpu.VMEM(checkpoint.shape, F32),
            pltpu.VMEM((1, pulses), F32),
        ),
        in_specs=[in_hbm] * 8,
        out_specs=(in_vmem, in_vmem),
        scratch_shapes=scratch,
        compiler_params=pltpu.CompilerParams(
            collective_id=0, has_side_effects=True, vmem_limit_bytes=60 * 2**20
        ),
    )(checkpoint, end_cotangent, buoyancy, moduli, yield_radius, mask, footprint, amplitude)
    return adjoint, sums.reshape(pulses)


def solution(mesh):
    placed = (
        P(None, "depth", "lat", None),
        P(None, "depth", "lat", None),
        P("depth", "lat", None),
        P(None, "depth", "lat", None),
        P("depth", "lat", None),
        P(None, "depth", "lat", None),
        P("lat", None),
        P(),
    )
    return jax.shard_map(
        functools.partial(per_device, (mesh.shape["depth"], mesh.shape["lat"])),
        mesh=mesh,
        in_specs=placed,
        out_specs=(P(None, "depth", "lat", None), P()),
        check_vma=False,
    )
```
